512 devices in a mesh: dp: 64 (over z_lo, x, y), feat: 8 (over z_hi, core).
Axes of the slice: x: 4, y: 8, z: 8 (z_hi: 4, z_lo: 2; z = z_hi * 2 + z_lo), core: 2. Of those that a mesh axis runs over, the one named last changes fastest.
Arguments:
- data: bfloat16 [32768, 28672], P('dp', 'feat'), may hold values from -100 to 100
- basis: float32 [8, 3584, 256], P('feat', 'dp'), may hold values from -6 to 6
Outputs:
- new_basis: float32 [8, 3584, 256], P('feat', 'dp')
The draws below stay inside these ranges and needn't reach their ends.
All inputs are finite; a program needn't handle non-finite values.
Results may differ from the reference program's by a relative error of at most 0.011.
Values may be sent and summed in bfloat16 or wider, within the bound.
A program may use at most 64 MiB of HBM per device.

```python
import math
import jax
import jax.numpy as jnp
from jax import lax

F = 28672
K = 256
FS = 3584
TOKENS = 32768
N_FEAT = 8


def draw_data(key, part):
    key = jax.random.fold_in(key, 7)
    key_a, key_b = jax.random.split(key, 2)
    position = jnp.arange(F, dtype=jnp.float32) / float(F)
    column_scale = jnp.exp(jax.random.uniform(key_b, (F,), jnp.float32, 0.0, math.log(10.0))) * jnp.power(3.0, 0.25 * position)
    values = jnp.clip(jax.random.normal(key_a, (TOKENS, F), jnp.float32), -6.0, 6.0)
    return (values * column_scale).astype(jnp.bfloat16)


def block_levels(stream_key, extent, pieces, smallest, high):
    def one(dim, blocks):
        draws = jax.random.uniform(jax.random.fold_in(jax.random.fold_in(stream_key, 6), dim), (blocks,), jnp.float32, smallest / len(pieces), high / len(pieces))
        return jnp.repeat(jnp.exp(draws), extent[dim] // blocks).reshape((-1,) + (1,) * (len(extent) - dim - 1))

    factor_of = one(*pieces[0])
    for cut in pieces[1:]:
        factor_of = factor_of * one(*cut)
    return factor_of


def bell_draw(stream_key, extent, spread, most, cuts=(), kind=jnp.bfloat16):
    drawn = spread * jax.random.normal(stream_key, extent, jnp.float32)
    if cuts:
        drawn = drawn * block_levels(stream_key, extent, cuts, -0.22, 0.18)
    return jnp.clip(drawn, -most, most).astype(kind)


def setup_inputs(seed: int = 0) -> dict:
    splits = jax.random.split(jax.random.key(seed), 3)
    return {
        "data": draw_data(jax.random.fold_in(splits[2], 71), 0),
        "basis": bell_draw(splits[1], (N_FEAT, FS, K), 1.0, 6.0, ((0, 8), (1, 64)), jnp.float32),
    }


def reference(data, basis):
    group_rows = F // N_FEAT
    flat = basis.reshape(F, K)
    rounded = flat.astype(jnp.bfloat16)
    total = jnp.zeros((data.shape[0], K), jnp.float32)
    for group in range(N_FEAT):
        lo = group * group_rows
        part = jnp.dot(data[:, lo:lo + group_rows].astype(jnp.float32), rounded[lo:lo + group_rows].astype(jnp.float32), preferred_element_type=jnp.float32)
        part = lax.optimization_barrier(part.astype(jnp.bfloat16))
        total = total + part.astype(jnp.float32)
    mixed = total.astype(jnp.bfloat16)
    product = lax.dot_general(data.astype(jnp.float32), mixed.astype(jnp.float32), (((0,), (0,)), ((), ())), preferred_element_type=jnp.float32)
    product = product / float(data.shape[0])
    gram = jnp.dot(product.T.astype(jnp.float32), product.astype(jnp.float32), precision=lax.Precision.HIGHEST, preferred_element_type=jnp.float32) / float(F)
    lower = jnp.linalg.cholesky(gram)
    result = lax.linalg.triangular_solve(lower, product, left_side=False, lower=True, transpose_a=True)
    return result.reshape(N_FEAT, group_rows, K)
```

```python
import jax
import jax.numpy as jnp
from jax import lax
from jax.experimental import pallas as pl
from jax.experimental.pallas import tpu as pltpu
from jax.sharding import PartitionSpec as P

F32 = jnp.float32
BF16 = jnp.bfloat16
MESH = pl.DeviceIdType.MESH
HI = lax.Precision.HIGHEST


class Cfg:
    def __init__(self, zl, x, y, zh, core, tokens, own=56, width=256, chunks=1):
        self.ZL, self.X, self.Y, self.ZH, self.C = zl, x, y, zh, core
        self.T, self.OWN, self.K, self.NC = tokens, own, width, chunks
        self.Z = zl * zh
        self.FE = zh * core
        self.DP = zl * x * y
        self.FS = own * self.DP
        self.CW = width // chunks
        self.TOTAL_T = tokens * self.DP
        self.F = self.FS * self.FE
        self.MX = x * core
        self.RX = width // self.MX
        self.RZ = self.RX * 2 // self.Z


ALPHA = 64


def reach(n, direction, sign):
    return n // 2 if direction == sign else n // 2 - 1


def offsets(n, sign):
    out = [0]
    for d in (1, -1):
        out += [d * h for h in range(1, reach(n, d, sign) + 1)]
    return out


def sgn(h):
    return (h > 0) - (h < 0)


class Part:
    def __init__(self, cfg, index):
        self.index = index
        self.sign = 1 if index == 0 else -1
        self.axes = ("y", "x") if index == 0 else ("x", "y")
        size = {"x": cfg.X, "y": cfg.Y}
        self.n = tuple(size[a] for a in self.axes)
        self.r0 = 0 if index == 0 else ALPHA
        self.rows = ALPHA if index == 0 else 2 * cfg.OWN - ALPHA
        self.events = [
            (a, b) for a in offsets(self.n[0], self.sign) for b in offsets(self.n[1], self.sign)
        ]
        self.id = {e: i for i, e in enumerate(self.events)}

    def can(self, axis, h, direction):
        return (h == 0 or sgn(h) == direction) and abs(h) + 1 <= reach(
            self.n[axis], direction, self.sign
        )


def comm_kernel(cfg, basis_ref, data_hbm, z_ref, gram_ref,
                xb, zs, zr, g, q, ypart, yr, yfull, zp, stage, rs, fin, zx_s, zx_r,
                g1, r1, s1, r2, s2, r3, s3, a2, gfull,
                xsem, zsem, ag_send, ag_recv, y_sem, rs_send, rs_recv, zx_sem,
                m1, m2, m3, m4, m5):
    X, Y, Z, ZL, C, NC, CW = cfg.X, cfg.Y, cfg.Z, cfg.ZL, cfg.C, cfg.NC, cfg.CW
    OWN = cfg.OWN
    dp = lax.axis_index("dp")
    feat = lax.axis_index("feat")
    my = dp % Y
    mx = (dp // Y) % X
    zl = dp // (X * Y)
    mc = feat % C
    mz = (feat // C) * ZL + zl
    me = {"x": mx, "y": my}

    def dev(ox=0, oy=0, oz=0, oc=0):
        x = (mx + ox + X) % X
        y = (my + oy + Y) % Y
        z = (mz + oz + Z) % Z
        c = (mc + oc) % C
        return {"dp": ((z % ZL) * X + x) * Y + y, "feat": (z // ZL) * C + c}

    partner = dev(oz=1 - 2 * zl)

    def rdma(src, dst, ssem, rsem, device):
        return pltpu.make_async_remote_copy(
            src_ref=src, dst_ref=dst, send_sem=ssem, recv_sem=rsem,
            device_id=device, device_id_type=MESH,
        )

    load = pltpu.make_async_copy(data_hbm, xb, xsem)
    load.start()

    own = basis_ref[0].astype(BF16).astype(F32)
    zs[...] = jnp.concatenate([own, jnp.zeros((64 - OWN, cfg.K), F32)], axis=0).astype(BF16)

    xc = [(ox, oc) for ox in range(X) for oc in range(C) if (ox, oc) != (0, 0)]
    fe = [(oz, oc) for oz in range(0, Z, ZL) for oc in range(C) if (oz, oc) != (0, 0)]
    peers = {(ox, 0, 0, oc) for ox, oc in xc}
    peers |= {(0, oy, 0, 0) for oy in range(1, Y)}
    peers |= {(0, 0, oz, 0) for oz in range(1, Z)}
    peers |= {(0, 0, oz, oc) for oz, oc in fe}
    barrier = pltpu.get_barrier_semaphore()
    for peer in sorted(peers):
        pl.semaphore_signal(barrier, inc=1, device_id=dev(*peer), device_id_type=MESH)
    pl.semaphore_wait(barrier, len(peers))

    swap = rdma(zs, zr, zsem.at[0], zsem.at[1], partner)
    swap.start()
    swap.wait_recv()
    other = zr[...].astype(F32)[:OWN]
    unit = jnp.concatenate(
        [jnp.where(zl == 0, own, other), jnp.where(zl == 0, other, own)], axis=0
    ).astype(BF16)
    for c in range(NC):
        g[c, mx, my] = unit[:, c * CW:(c + 1) * CW]

    parts = [Part(cfg, 0), Part(cfg, 1)]
    pending = [swap]

    def near(axis, direction):
        return dev(ox=direction) if axis == "x" else dev(oy=direction)

    def origin(part, e):
        at = {}
        for k in range(2):
            n = part.n[k]
            at[part.axes[k]] = (me[part.axes[k]] - e[k] + n) % n
        return at["x"], at["y"]

    def gather(c):
        todo = [(abs(e[0]) + abs(e[1]), p.index, p.id[e], p, e) for p in parts for e in p.events]
        todo.sort(key=lambda t: t[:3])
        count = [0, 0]
        for _, pi, ei, p, e in todo:
            ux, uy = origin(p, e)
            slot = g.at[c, ux, uy, pl.ds(p.r0, p.rows)]
            if e != (0, 0):
                rdma(slot, slot, ag_send.at[c, pi, 0], ag_recv.at[c, pi, ei], partner).wait_recv()
            for k in range(2):
                if k == 0 and e[1] != 0:
                    continue
                for d in (1, -1):
                    if not p.can(k, e[k], d):
                        continue
                    to = (e[0] + d, e[1]) if k == 0 else (e[0], e[1] + d)
                    cp = rdma(slot, slot, ag_send.at[c, pi, count[pi]],
                              ag_recv.at[c, pi, p.id[to]], near(p.axes[k], d))
                    count[pi] += 1
                    cp.start()
                    pending.append(cp)

    def arrange(c):
        def pair(i, carry):
            ux = i // (Y // 2)
            uy = (i % (Y // 2)) * 2
            a = g[c, ux, uy].astype(F32)
            b = g[c, ux, uy + 1].astype(F32)
            for zz in range(ZL):
                rows = jnp.concatenate(
                    [a[zz * OWN:(zz + 1) * OWN], b[zz * OWN:(zz + 1) * OWN]], axis=0
                ).astype(BF16)
                at = pl.multiple_of(((zz * X + ux) * Y + uy) * OWN, 2 * OWN)
                q[c, pl.ds(at, 2 * OWN)] = rows
            return carry
        lax.fori_loop(0, X * Y // 2, pair, 0)

    TS = cfg.T // cfg.FE

    def sum_y(c):
        part = jnp.dot(xb[...], q[c], preferred_element_type=F32).astype(BF16)
        for k in range(cfg.FE):
            ypart[c, k] = part[k * TS:(k + 1) * TS]
        copies = []
        for i, (oz, oc) in enumerate(fe):
            to = dev(oz=oz, oc=oc)
            cp = rdma(ypart.at[c, to["feat"]], yr.at[c, i], y_sem.at[c, 0, i], y_sem.at[c, 1, i], to)
            cp.start()
            copies.append(cp)
        total = ypart[c, feat].astype(F32)
        for i, cp in enumerate(copies):
            cp.wait_recv()
            total = total + yr[c, i].astype(F32)
        yfull[c, feat] = total.astype(BF16)
        pending.extend(copies)
        copies = []
        for i, (oz, oc) in enumerate(fe):
            cp = rdma(yfull.at[c, feat], yfull.at[c, feat], y_sem.at[c, 2, i], y_sem.at[c, 3, i],
                      dev(oz=oz, oc=oc))
            cp.start()
            copies.append(cp)
        for i, (oz, oc) in enumerate(fe):
            frm = dev(oz=-oz, oc=oc)["feat"]
            rdma(yfull.at[c, frm], yfull.at[c, frm], y_sem.at[c, 2, i], y_sem.at[c, 3, i],
                 dev(oz=oz, oc=oc)).wait_recv()
        pending.extend(copies)

    def product(c):
        y = yfull[c].reshape(cfg.T, CW)
        zp[c] = lax.dot_general(xb[...], y, (((0,), (0,)), ((), ())), preferred_element_type=F32)

    def scatter(c):
        todo = [(-abs(e[0]) - abs(e[1]), p.index, p.id[e], p, e) for p in parts for e in p.events]
        todo.sort(key=lambda t: t[:3])
        for _, pi, ei, p, e in todo:
            ux, uy = origin(p, e)
            at0 = pl.multiple_of((ux * Y + uy) * OWN, OWN)
            at1 = pl.multiple_of((X * Y + ux * Y + uy) * OWN, OWN)
            if pi == 0:
                v = jnp.concatenate(
                    [zp[c, pl.ds(at0, OWN)], zp[c, pl.ds(at1, ALPHA - OWN)]], axis=0
                )
            else:
                v = zp[c, pl.ds(at1 + (ALPHA - OWN), p.rows)]
            arrivals = []
            for d in (1, -1):
                if p.can(1, e[1], d):
                    arrivals.append((e[0], e[1] + d))
                if e[1] == 0 and p.can(0, e[0], d):
                    arrivals.append((e[0] + d, 0))
            for a in arrivals:
                slot = rs.at[c, pi, p.id[a], pl.ds(0, p.rows)]
                rdma(slot, slot, rs_send.at[c, pi, 0], rs_recv.at[c, pi, p.id[a]], partner).wait_recv()
                v = v + slot[...].astype(F32)
            if e == (0, 0):
                fin[c, pl.ds(p.r0, p.rows)] = v
                continue
            k = 1 if e[1] != 0 else 0
            stage[c, pi, ei, pl.ds(0, p.rows)] = v.astype(BF16)
            cp = rdma(stage.at[c, pi, ei, pl.ds(0, p.rows)], rs.at[c, pi, ei, pl.ds(0, p.rows)],
                      rs_send.at[c, pi, ei], rs_recv.at[c, pi, ei], near(p.axes[k], -sgn(e[k])))
            cp.start()
            pending.append(cp)
        lo = fin[c, pl.ds(0, OWN)]
        hi = fin[c, pl.ds(OWN, OWN)]
        zx_s[c] = jnp.where(zl == 0, hi, lo)
        cp = rdma(zx_s.at[c], zx_r.at[c], zx_sem.at[c, 0], zx_sem.at[c, 1], partner)
        cp.start()
        pending.append(cp)
        cp.wait_recv()
        return (jnp.where(zl == 0, lo, hi) + zx_r[c]) / float(cfg.TOTAL_T)

    def gram_sum(z):
        gl = lax.dot_general(z, z, (((0,), (0,)), ((), ())), precision=HI, preferred_element_type=F32)
        g1[0] = gl[:, :128]
        g1[1] = gl[:, 128:]
        RX, RZ = cfg.RX, cfg.RZ
        m = mx * C + mc

        def exchange(offs, sems, src, dst, wait):
            copies = []
            for i, off in enumerate(offs):
                cp = rdma(src(off), dst(i), sems.at[0, i], sems.at[1, i], dev(*off))
                cp.start()
                copies.append(cp)
            for i, off in enumerate(offs):
                back = wait(i, off)
                rdma(back, back, sems.at[0, i], sems.at[1, i], dev(*off)).wait_recv()
            pending.extend(copies)

        xoff = [(ox, 0, 0, oc) for ox, oc in xc]
        zoff = [(0, 0, oz, 0) for oz in range(1, Z)]
        yoff = [(0, oy, 0, 0) for oy in range(1, Y)]

        def rows1(off):
            t = ((mx + off[0] + X) % X) * C + (mc + off[3]) % C
            return pl.ds(pl.multiple_of(t * RX, RX), RX)

        mine = pl.ds(pl.multiple_of(m * RX, RX), RX)
        exchange(xoff, m1, lambda off: g1.at[:, rows1(off)], lambda i: r1.at[i], lambda i, off: r1.at[i])
        total = g1[:, mine]
        for i in range(len(xoff)):
            total = total + r1[i]
        s1[...] = total

        def tile(z):
            return z % 2, pl.ds(pl.multiple_of((z // 2) * RZ, RZ), RZ)

        def tile_to(off):
            return tile((mz + off[2] + Z) % Z)

        exchange(zoff, m2, lambda off: s1.at[tile_to(off)], lambda i: r2.at[i], lambda i, off: r2.at[i])
        half, rows = tile(mz)
        total = s1[half, rows]
        for i in range(len(zoff)):
            total = total + r2[i]
        s2[...] = total
        exchange(yoff, m3, lambda off: s2, lambda i: r3.at[i], lambda i, off: r3.at[i])
        total = s2[...]
        for i in range(len(yoff)):
            total = total + r3[i]
        a2[half, rows] = total
        own_tile = a2.at[half, rows]
        exchange(zoff, m4, lambda off: own_tile, lambda i: own_tile,
                 lambda i, off: a2.at[tile((mz - off[2] + Z) % Z)])
        gfull[:, mine] = a2[...]
        exchange(xoff, m5, lambda off: a2, lambda i: gfull.at[:, mine],
                 lambda i, off: gfull.at[:, rows1((-off[0], 0, 0, off[3]))])
        gram_ref[...] = gfull[...]

    for c in range(NC):
        gather(c)
    load.wait()
    for c in range(NC):
        arrange(c)
        sum_y(c)
        product(c)
    cols = [scatter(c) for c in range(NC)]
    z = jnp.concatenate(cols, axis=1) if NC > 1 else cols[0]
    z_ref[...] = z
    gram_sum(z)
    for cp in pending:
        cp.wait_send()


def communicate(cfg, basis, data, vmem=48 << 20):
    NC, CW, X, Y = cfg.NC, cfg.CW, cfg.X, cfg.Y
    K, OWN, T, FS = cfg.K, cfg.OWN, cfg.T, cfg.FS
    ev = X * Y
    nf, nx, nz, ny = cfg.FE - 1, cfg.MX - 1, cfg.Z - 1, Y - 1
    VM = pltpu.VMEM
    DMA = pltpu.SemaphoreType.DMA
    scratch = [
        VM((T, FS), BF16), VM((64, K), BF16), VM((64, K), BF16),
        VM((NC, X, Y, 2 * OWN, CW), BF16), VM((NC, FS, CW), BF16),
        VM((NC, cfg.FE, T // cfg.FE, CW), BF16), VM((NC, nf, T // cfg.FE, CW), BF16),
        VM((NC, cfg.FE, T // cfg.FE, CW), BF16),
        VM((NC, FS, CW), F32), VM((NC, 2, ev, ALPHA, CW), BF16), VM((NC, 2, ev, ALPHA, CW), BF16),
        VM((NC, 2 * OWN, CW), F32), VM((NC, OWN, CW), F32), VM((NC, OWN, CW), F32),
        VM((2, K, 128), F32), VM((nx, 2, cfg.RX, 128), F32), VM((2, cfg.RX, 128), F32),
        VM((nz, cfg.RZ, 128), F32), VM((cfg.RZ, 128), F32), VM((ny, cfg.RZ, 128), F32),
        VM((cfg.RZ, 128), F32), VM((2, cfg.RX, 128), F32), VM((2, K, 128), F32),
        DMA, DMA((2,)), DMA((NC, 2, ev)), DMA((NC, 2, ev)), DMA((NC, 4, nf)),
        DMA((NC, 2, ev)), DMA((NC, 2, ev)), DMA((NC, 2)),
        DMA((2, nx)), DMA((2, nz)), DMA((2, ny)), DMA((2, nz)), DMA((2, nx)),
    ]

    def body(*refs):
        comm_kernel(cfg, *refs)

    return pl.pallas_call(
        body,
        out_shape=(
            jax.ShapeDtypeStruct((OWN, K), F32),
            jax.ShapeDtypeStruct((2, K, 128), F32),
        ),
        in_specs=[pl.BlockSpec(memory_space=pltpu.VMEM), pl.BlockSpec(memory_space=pl.ANY)],
        out_specs=(pl.BlockSpec(memory_space=pltpu.VMEM), pl.BlockSpec(memory_space=pltpu.VMEM)),
        scratch_shapes=scratch,
        compiler_params=pltpu.CompilerParams(
            collective_id=0, has_side_effects=True, vmem_limit_bytes=vmem
        ),
        name="power_step",
    )(basis, data)


def split3(v):
    h = v.astype(BF16)
    r = v - h.astype(F32)
    m = r.astype(BF16)
    return h, m, (r - m.astype(F32)).astype(BF16)


def factor_kernel(scale, B, z_ref, gram_ref, out_ref, w):
    own, K = z_ref.shape
    w[:, 0:128] = gram_ref[0] * scale
    w[:, 128:256] = gram_ref[1] * scale
    w[:, 256:384] = jnp.concatenate([z_ref[...], jnp.zeros((128 - own, K), F32)], axis=0).T
    sub = lax.broadcasted_iota(jnp.int32, (8, 128), 0)
    G = B // 8
    for blk in range(K // B):
        r0 = blk * B
        t0 = r0 // 128
        tiles = list(range(t0, 3))
        v = [[w[r0 + 8 * s:r0 + 8 * s + 8, t * 128:(t + 1) * 128] for t in tiles] for s in range(G)]
        scales = []
        for s0 in range(G):
            lane = (r0 + 8 * s0) % 128
            col = {
                s: [jnp.broadcast_to(v[s][0][:, lane + k:lane + k + 1], (8, 128)) for k in range(8)]
                for s in range(s0, G)
            }
            dvec = jnp.zeros((8, 128), F32)
            for j in range(8):
                prow = [jnp.broadcast_to(v[s0][t][j:j + 1], (8, 128)) for t in range(len(tiles))]
                pcol = [jnp.broadcast_to(col[s0][k][j:j + 1], (8, 128)) if k >= j else None
                        for k in range(8)]
                inv = 1.0 / pcol[j]
                dvec = jnp.where(sub == j, pcol[j], dvec)
                for s in range(s0, G):
                    mult = col[s][j] * inv
                    if s == s0:
                        mult = jnp.where(sub > j, mult, 0.0)
                    for k in range(j + 1, 8):
                        col[s][k] = col[s][k] - mult * pcol[k]
                    for t in range(len(tiles)):
                        v[s][t] = v[s][t] - mult * prow[t]
            scales.append(lax.rsqrt(dvec))
        for s in range(G):
            for t in range(len(tiles)):
                v[s][t] = v[s][t] * scales[s]
                if tiles[t] == 2:
                    w[r0 + 8 * s:r0 + 8 * s + 8, 256:384] = v[s][t]
        if blk + 1 < K // B:
            rows = jnp.concatenate([jnp.concatenate(v[s], axis=1) for s in range(G)], axis=0)
            h, m, l = split3(rows)
            n0 = ((r0 + B) // 128) * 128 - t0 * 128
            left = jnp.concatenate([h, h, m, m, h, l], axis=0)
            right = jnp.concatenate([h, m, h, m, l, h], axis=0)
            upd = lax.dot_general(left[:, n0:K - t0 * 128], right[:, n0:], (((0,), (0,)), ((), ())),
                                  preferred_element_type=F32)
            c0 = t0 * 128 + n0
            w[r0 + B:K, c0:384] = w[r0 + B:K, c0:384] - upd[r0 + B - c0:]
    out_ref[0] = w[:, 256:384].T[:own]


def factor(cfg, z, gram, block=32):
    def body(z_ref, gram_ref, out_ref, w):
        factor_kernel(1.0 / float(cfg.F), block, z_ref, gram_ref, out_ref, w)

    return pl.pallas_call(
        body,
        out_shape=jax.ShapeDtypeStruct((1, cfg.OWN, cfg.K), F32),
        in_specs=[pl.BlockSpec(memory_space=pltpu.VMEM)] * 2,
        out_specs=pl.BlockSpec(memory_space=pltpu.VMEM),
        scratch_shapes=[pltpu.VMEM((cfg.K, 384), F32)],
        name="factor_rows",
    )(z, gram)


def solution(mesh):
    cfg = Cfg(zl=2, x=4, y=8, zh=4, core=2, tokens=512)

    def per_device(data, basis):
        z, gram = communicate(cfg, basis, data)
        return factor(cfg, z, gram)

    return jax.shard_map(
        per_device, mesh=mesh, in_specs=(P("dp", "feat"), P("feat", "dp", None)),
        out_specs=P("feat", "dp", None), check_vma=False,
    )
```

```python
import jax
import jax.numpy as jnp
from jax import lax
from jax.experimental import pallas as pl
from jax.experimental.pallas import tpu as pltpu
from jax.sharding import PartitionSpec as P

F32 = jnp.float32
BF16 = jnp.bfloat16
MESH = pl.DeviceIdType.MESH
HI = lax.Precision.HIGHEST


class Cfg:
    def __init__(self, zl, x, y, zh, core, tokens, own=56, width=256, alpha=80,
                 trees=("skip", "skip")):
        self.ZL, self.X, self.Y, self.ZH, self.C = zl, x, y, zh, core
        self.T, self.OWN, self.K = tokens, own, width
        self.Z = zl * zh
        self.FE = zh * core
        self.DP = zl * x * y
        self.FS = own * self.DP
        self.TOTAL_T = tokens * self.DP
        self.F = self.FS * self.FE
        self.MX = x * core
        self.RX = width // self.MX
        self.RZ = self.RX * 2 // self.Z
        self.alpha = alpha
        self.beta = 2 * own - alpha
        self.trees = [tree(y, kind) for kind in trees]


def tree(n, kind):
    up, down = n // 2, n // 2 - 1
    out = {}
    for h in range(1, up + 1):
        for d in ([1, -1] if h <= down else [1]):
            out[d * h] = d * (0 if kind == "direct" or h <= 2 else 2)
    return out


def position(h, n):
    s = (h + n + n // 2 - 1) % n - (n // 2 - 1)
    up = (s + n // 2 - 1) // (n // 2)
    return 2 * s * (2 * up - 1) - up


def comm_kernel(cfg, basis_ref, data_hbm, z_ref, gram_ref,
                xb, bb, zs, zr, ga, gb, q, ypart, ysib, ypair, yr, yfull, zp, sax, rax, say, ray, sby, rby, sbx, rbx, fin, zx_s, zx_r,
                g1, r1, s1, r2, s2, r3, s3, a2, gfull,
                xsem, bsem, zsem, gsem, y_sem, ssem, zx_sem,
                m1, m2, m3, m4, m5):
    X, Y, Z, ZL, ZH, C = cfg.X, cfg.Y, cfg.Z, cfg.ZL, cfg.ZH, cfg.C
    OWN, A = cfg.OWN, cfg.alpha
    dp = lax.axis_index("dp")
    feat = lax.axis_index("feat")
    my = dp % Y
    mx = (dp // Y) % X
    zl = dp // (X * Y)
    mc = feat % C
    mz = (feat // C) * ZL + zl
    me = {"x": mx, "y": my}

    def dev(ox=0, oy=0, oz=0, oc=0):
        x = (mx + ox + X) % X
        y = (my + oy + Y) % Y
        z = (mz + oz + Z) % Z
        c = (mc + oc) % C
        return {"dp": ((z % ZL) * X + x) * Y + y, "feat": (z // ZL) * C + c}

    partner = dev(oz=1 - 2 * zl)

    def rdma(src, dst, ssem, rsem, device):
        return pltpu.make_async_remote_copy(
            src_ref=src, dst_ref=dst, send_sem=ssem, recv_sem=rsem,
            device_id=device, device_id_type=MESH,
        )

    load = pltpu.make_async_copy(data_hbm, xb, xsem)
    load.start()

    fetch = pltpu.make_async_copy(basis_ref, bb, bsem)
    fetch.start()
    xc = [(ox, oc) for ox in range(X) for oc in range(C) if (ox, oc) != (0, 0)]
    fe = [(oz, oc) for oz in range(0, Z, ZL) for oc in range(C) if (oz, oc) != (0, 0)]
    peers = {(0, 0, oz, oc) for oz, oc in fe}
    peers |= {(ox, 0, 0, oc) for ox, oc in xc}
    peers |= {(0, oy, 0, 0) for oy in range(1, Y)}
    peers |= {(0, 0, oz, 0) for oz in range(1, Z)}
    barrier = pltpu.get_barrier_semaphore()
    for peer in sorted(peers):
        pl.semaphore_signal(barrier, inc=1, device_id=dev(*peer), device_id_type=MESH)
    fetch.wait()
    own = bb[0].astype(BF16).astype(F32)
    zs[...] = jnp.concatenate([own, jnp.zeros((64 - OWN, cfg.K), F32)], axis=0).astype(BF16)
    pl.semaphore_wait(barrier, len(peers))

    swap = rdma(zs, zr, zsem.at[0], zsem.at[1], partner)
    swap.start()
    swap.wait_recv()
    other = zr[...].astype(F32)[:OWN]
    unit = jnp.concatenate(
        [jnp.where(zl == 0, own, other), jnp.where(zl == 0, other, own)], axis=0
    ).astype(BF16)
    pos = lambda h: position(h, Y)
    ga[mx, 0] = unit[:A]
    gb[my, mx] = unit[A:]
    pending = [swap]
    xo = list(range(1, X))
    ta, tb = cfg.trees
    order = sorted(ta, key=pos)
    groups = [[0], [h for h in order if abs(h) <= 2], [h for h in order if abs(h) > 2]]
    groups = [h for h in groups if h]

    def below(t, h):
        return sorted([k for k, v in t.items() if v == h], key=lambda k: -abs(k))

    def send(src, dst, sems, i, device):
        cp = rdma(src, dst, sems.at[0, i], sems.at[1, i], device)
        cp.start()
        pending.append(cp)

    def arrived(dst, sems, i):
        rdma(dst, dst, sems.at[0, i], sems.at[1, i], partner).wait_recv()

    def flush():
        while pending:
            pending.pop().wait_send()

    def span(group):
        return pl.ds(pos(group[0]), len(group))

    def gather():
        ax, ay, bx, by = [gsem.at[i] for i in range(4)]
        for i, o in enumerate(xo):
            send(gb.at[my, mx], gb.at[my, mx], bx, i, dev(ox=o))

        def along_y_a(h):
            for k in below(ta, h):
                send(ga.at[mx, pos(h)], ga.at[mx, pos(k)], ay, pos(k), dev(oy=k - h))

        def along_x_a(n):
            part = ga.at[mx, span(groups[n])]
            for i, o in enumerate(xo):
                send(part, part, ax, n * X + i, dev(ox=o))

        def along_y_b(h):
            part = gb.at[(my - h + Y) % Y]
            for k in below(tb, h):
                send(part, part, by, pos(k), dev(oy=k - h))

        def wait_b(h):
            arrived(gb.at[(my - h + Y) % Y], by, pos(h))

        along_y_a(0)
        along_x_a(0)
        for i, o in enumerate(xo):
            arrived(gb.at[my, (mx - o + X) % X], bx, i)
        along_y_b(0)
        for h in sorted(groups[1], key=lambda h: -abs(h)):
            arrived(ga.at[mx, pos(h)], ay, pos(h))
            along_y_a(h)
        along_x_a(1)
        for h in sorted(groups[1], key=lambda h: -abs(h)):
            wait_b(h)
            along_y_b(h)
        for n in range(2, len(groups)):
            for h in groups[n]:
                arrived(ga.at[mx, pos(h)], ay, pos(h))
            along_x_a(n)
            for h in groups[n]:
                wait_b(h)
        for n in range(len(groups)):
            for i, o in enumerate(xo):
                arrived(ga.at[(mx - o + X) % X, span(groups[n])], ax, n * X + i)

    def arrange():
        def pair(i, carry):
            ux = i // (Y // 2)
            uy = (i % (Y // 2)) * 2
            a, b = [
                jnp.concatenate([ga[ux, pos(my - v + Y)].astype(F32), gb[v, ux].astype(F32)], axis=0)
                for v in (uy, uy + 1)
            ]
            for zz in range(ZL):
                rows = jnp.concatenate(
                    [a[zz * OWN:(zz + 1) * OWN], b[zz * OWN:(zz + 1) * OWN]], axis=0
                ).astype(BF16)
                at = pl.multiple_of(((zz * X + ux) * Y + uy) * OWN, 2 * OWN)
                q[pl.ds(at, 2 * OWN)] = rows
            return carry
        lax.fori_loop(0, X * Y // 2, pair, 0)

    TS = cfg.T // cfg.FE

    def sum_y():
        part = jnp.dot(xb[...], q[...], preferred_element_type=F32).astype(BF16)
        for h in range(C):
            for k in range(ZH):
                lo = (h * ZH + k) * TS
                ypart[h, k] = part[lo:lo + TS]
        mh = mz // ZL
        for h in range(1, C):
            cp = rdma(ypart.at[(mc + h) % C], ysib, y_sem.at[0, 0], y_sem.at[1, 0],
                      dev(oc=h))
            cp.start()
            pending.append(cp)
            cp.wait_recv()
        pair = ypart[mc].astype(F32) + ysib[...].astype(F32)
        ypair[...] = pair.astype(BF16)
        zoff = list(range(ZL, Z, ZL))
        for i, oz in enumerate(zoff):
            to = (mz + oz) % Z // ZL
            cp = rdma(ypair.at[to], yr.at[i], y_sem.at[0, 1 + i], y_sem.at[1, 1 + i],
                      dev(oz=oz))
            cp.start()
            pending.append(cp)
        flush()
        total = ypart[mc, mh].astype(F32) + ysib[mh].astype(F32)
        for i in range(len(zoff)):
            rdma(yr.at[i], yr.at[i], y_sem.at[0, 1 + i], y_sem.at[1, 1 + i],
                 partner).wait_recv()
            total = total + yr[i].astype(F32)
        yfull[mc, mh] = total.astype(BF16)
        slot = yfull.at[mc, mh]
        for i, oz in enumerate(zoff):
            cp = rdma(slot, slot, y_sem.at[2, 1 + i], y_sem.at[3, 1 + i], dev(oz=oz))
            cp.start()
            pending.append(cp)
        for i, oz in enumerate(zoff):
            slot = yfull.at[mc, (mz + Z - oz) % Z // ZL]
            rdma(slot, slot, y_sem.at[2, 1 + i], y_sem.at[3, 1 + i], partner).wait_recv()
        slot = yfull.at[mc]
        for h in range(1, C):
            cp = rdma(slot, slot, y_sem.at[2, 0], y_sem.at[3, 0], dev(oc=h))
            cp.start()
            pending.append(cp)
            slot = yfull.at[(mc + h) % C]
            rdma(slot, slot, y_sem.at[2, 0], y_sem.at[3, 0], dev(oc=h)).wait_recv()

    def product():
        y = yfull[...].reshape(cfg.T, cfg.K)
        zp[...] = lax.dot_general(xb[...], y, (((0,), (0,)), ((), ())), preferred_element_type=F32)

    def rows_a(hx, hy):
        u = ((mx - hx + X) % X) * Y + (my - hy + Y) % Y
        at0 = pl.multiple_of(u * OWN, OWN)
        at1 = pl.multiple_of((X * Y + u) * OWN, OWN)
        return jnp.concatenate([zp[pl.ds(at0, OWN)], zp[pl.ds(at1, A - OWN)]], axis=0)

    def rows_b(hx, hy):
        u = ((mx - hx + X) % X) * Y + (my - hy + Y) % Y
        return zp[pl.ds(pl.multiple_of((X * Y + u) * OWN + (A - OWN), 8), cfg.beta)]

    def scatter():
        ax, ay, bx, by = [ssem.at[i] for i in range(4)]
        def out_x_a(n):
            for i, o in enumerate(xo):
                for h in groups[n]:
                    sax[i, pos(h)] = rows_a(o, h).astype(BF16)
                part = span(groups[n])
                send(sax.at[i, part], rax.at[i, part], ax, n * X + i, dev(ox=-o))

        def out_y_b(h):
            for hx in range(X):
                v = rows_b(hx, h)
                for k in below(tb, h):
                    v = v + rby[pos(k), hx].astype(F32)
                sby[pos(h), hx] = v.astype(BF16)
            send(sby.at[pos(h)], rby.at[pos(h)], by, pos(h), dev(oy=tb[h] - h))

        def sum_a(h):
            v = rows_a(0, h)
            for i in range(len(xo)):
                v = v + rax[i, pos(h)].astype(F32)
            for k in below(ta, h):
                v = v + ray[pos(k)].astype(F32)
            return v

        def out_y_a(h):
            say[pos(h)] = sum_a(h).astype(BF16)
            send(say.at[pos(h)], ray.at[pos(h)], ay, pos(h), dev(oy=ta[h] - h))

        def wait_x_a(n):
            for i in range(len(xo)):
                arrived(rax.at[i, span(groups[n])], ax, n * X + i)

        def wait_y(buf, sems, t, h):
            for k in below(t, h):
                arrived(buf.at[pos(k)], sems, pos(k))

        far = [h for n in range(2, len(groups)) for h in groups[n]]
        mid = sorted(groups[1], key=lambda h: -abs(h))
        for h in far:
            out_y_b(h)
        for n in range(2, len(groups)):
            out_x_a(n)
        for h in mid:
            if not below(tb, h):
                out_y_b(h)
        out_x_a(1)
        out_x_a(0)
        for n in range(2, len(groups)):
            wait_x_a(n)
        for h in far:
            out_y_a(h)
        for h in mid:
            if below(tb, h):
                wait_y(rby, by, tb, h)
                out_y_b(h)
        wait_x_a(1)
        for h in mid:
            if not below(ta, h):
                out_y_a(h)
        for h in mid:
            if below(ta, h):
                wait_y(ray, ay, ta, h)
                out_y_a(h)
        wait_y(rby, by, tb, 0)
        for i, o in enumerate([0] + xo):
            v = rows_b(o, 0)
            for k in below(tb, 0):
                v = v + rby[pos(k), o].astype(F32)
            if o == 0:
                last_b = v
            else:
                sbx[i - 1] = v.astype(BF16)
                send(sbx.at[i - 1], rbx.at[i - 1], bx, i - 1, dev(ox=-o))
        wait_x_a(0)
        wait_y(ray, ay, ta, 0)
        fin[pl.ds(0, A)] = sum_a(0)
        for i in range(len(xo)):
            arrived(rbx.at[i], bx, i)
            last_b = last_b + rbx[i].astype(F32)
        fin[pl.ds(A, cfg.beta)] = last_b
        lo = fin[pl.ds(0, OWN)]
        hi = fin[pl.ds(OWN, OWN)]
        zx_s[...] = jnp.where(zl == 0, hi, lo)
        cp = rdma(zx_s, zx_r, zx_sem.at[0], zx_sem.at[1], partner)
        cp.start()
        pending.append(cp)
        flush()
        cp.wait_recv()
        return (jnp.where(zl == 0, lo, hi) + zx_r[...]) / float(cfg.TOTAL_T)

    def gram_sum(z):
        gl = lax.dot_general(z, z, (((0,), (0,)), ((), ())), precision=HI, preferred_element_type=F32)
        g1[0] = gl[:, :128]
        g1[1] = gl[:, 128:]
        RX, RZ = cfg.RX, cfg.RZ
        m = mc * X + mx

        def exchange(offs, sems, src, dst, wait):
            copies = []
            for i, off in enumerate(offs):
                cp = rdma(src(off), dst(i), sems.at[0, i], sems.at[1, i], dev(*off))
                cp.start()
                copies.append(cp)
            flush()
            for i, off in enumerate(offs):
                back = wait(i, off)
                rdma(back, back, sems.at[0, i], sems.at[1, i], dev(*off)).wait_recv()
            pending.extend(copies)

        xoff = [(ox, 0, 0, oc) for ox, oc in xc]
        zoff = [(0, 0, oz, 0) for oz in range(1, Z)]
        yoff = [(0, oy, 0, 0) for oy in range(1, Y)]

        def rows1(off):
            t = ((mc + off[3]) % C) * X + (mx + off[0] + X) % X
            return pl.ds(pl.multiple_of(t * RX, RX), RX)

        mine = pl.ds(pl.multiple_of(m * RX, RX), RX)
        exchange(xoff, m1, lambda off: g1.at[:, rows1(off)], lambda i: r1.at[i], lambda i, off: r1.at[i])
        total = g1[:, mine]
        for i in range(len(xoff)):
            total = total + r1[i]
        s1[...] = total

        def tile(z):
            return z % 2, pl.ds(pl.multiple_of((z // 2) * RZ, RZ), RZ)

        def tile_to(off):
            return tile((mz + off[2] + Z) % Z)

        exchange(zoff, m2, lambda off: s1.at[tile_to(off)], lambda i: r2.at[i], lambda i, off: r2.at[i])
        half, rows = tile(mz)
        total = s1[half, rows]
        for i in range(len(zoff)):
            total = total + r2[i]
        s2[...] = total
        exchange(yoff, m3, lambda off: s2, lambda i: r3.at[i], lambda i, off: r3.at[i])
        total = s2[...]
        for i in range(len(yoff)):
            total = total + r3[i]
        a2[half, rows] = total
        own_tile = a2.at[half, rows]
        exchange(zoff, m4, lambda off: own_tile, lambda i: own_tile,
                 lambda i, off: a2.at[tile((mz - off[2] + Z) % Z)])
        gfull[:, mine] = a2[...]
        near = [off for off in xoff if off[3] == 0]
        exchange(near, m5, lambda off: a2, lambda i: gfull.at[:, mine],
                 lambda i, off: gfull.at[:, rows1((-off[0], 0, 0, 0))])
        for h in range(1, C):
            def half(c):
                return gfull.at[:, pl.ds(pl.multiple_of(c % C * (X * RX), X * RX), X * RX)]
            cp = rdma(half(mc), half(mc), m5.at[0, len(near)], m5.at[1, len(near)], dev(oc=h))
            cp.start()
            pending.append(cp)
            rdma(half(mc + h), half(mc + h), m5.at[0, len(near)], m5.at[1, len(near)],
                 dev(oc=h)).wait_recv()
        gram_ref[...] = gfull[...]

    gather()
    load.wait()
    arrange()
    sum_y()
    product()
    z = scatter()
    z_ref[...] = z
    gram_sum(z)
    flush()


def communicate(cfg, basis, data, vmem=48 << 20):
    X, Y, Z, C, ZH = cfg.X, cfg.Y, cfg.Z, cfg.C, cfg.ZH
    K, OWN, T, FS, A, B = cfg.K, cfg.OWN, cfg.T, cfg.FS, cfg.alpha, cfg.beta
    TS = T // cfg.FE
    nx, nz, ny = cfg.MX - 1, Z - 1, Y - 1
    VM = pltpu.VMEM
    DMA = pltpu.SemaphoreType.DMA
    scratch = [
        VM((T, FS), BF16), VM((1, OWN, K), F32), VM((64, K), BF16), VM((64, K), BF16),
        VM((X, Y, A, K), BF16), VM((Y, X, B, K), BF16), VM((FS, K), BF16),
        VM((C, ZH, TS, K), BF16), VM((ZH, TS, K), BF16), VM((ZH, TS, K), BF16),
        VM((ZH, TS, K), BF16), VM((C, ZH, TS, K), BF16),
        VM((FS, K), F32), VM((X - 1, Y, A, K), BF16), VM((X - 1, Y, A, K), BF16),
        VM((Y, A, K), BF16), VM((Y, A, K), BF16), VM((Y, X, B, K), BF16), VM((Y, X, B, K), BF16),
        VM((X - 1, B, K), BF16), VM((X - 1, B, K), BF16),
        VM((2 * OWN, K), F32), VM((OWN, K), F32), VM((OWN, K), F32),
        VM((2, K, 128), F32), VM((nx, 2, cfg.RX, 128), F32), VM((2, cfg.RX, 128), F32),
        VM((nz, cfg.RZ, 128), F32), VM((cfg.RZ, 128), F32), VM((ny, cfg.RZ, 128), F32),
        VM((cfg.RZ, 128), F32), VM((2, cfg.RX, 128), F32), VM((2, K, 128), F32),
        DMA, DMA, DMA((2,)), DMA((4, 2, 3 * X + Y)), DMA((4, 1 + ZH)),
        DMA((4, 2, 3 * X + Y)), DMA((2,)),
        DMA((2, nx)), DMA((2, nz)), DMA((2, ny)), DMA((2, nz)), DMA((2, nx)),
    ]

    def body(*refs):
        comm_kernel(cfg, *refs)

    return pl.pallas_call(
        body,
        out_shape=(
            jax.ShapeDtypeStruct((OWN, K), F32),
            jax.ShapeDtypeStruct((2, K, 128), F32),
        ),
        in_specs=[pl.BlockSpec(memory_space=pltpu.HBM)] * 2,
        out_specs=(pl.BlockSpec(memory_space=pltpu.VMEM), pl.BlockSpec(memory_space=pltpu.VMEM)),
        scratch_shapes=scratch,
        compiler_params=pltpu.CompilerParams(
            collective_id=0, has_side_effects=True, vmem_limit_bytes=vmem
        ),
        name="power_step",
    )(
        pltpu.with_memory_space_constraint(basis, pltpu.HBM),
        pltpu.with_memory_space_constraint(data, pltpu.HBM),
    )


def split3(v):
    h = v.astype(BF16)
    r = v - h.astype(F32)
    m = r.astype(BF16)
    return h, m, (r - m.astype(F32)).astype(BF16)


def factor_kernel(scale, B, z_ref, gram_ref, out_ref, w):
    own, K = z_ref.shape
    w[:, 0:128] = gram_ref[0] * scale
    w[:, 128:256] = gram_ref[1] * scale
    w[:, 256:384] = jnp.concatenate([z_ref[...], jnp.zeros((128 - own, K), F32)], axis=0).T
    sub = lax.broadcasted_iota(jnp.int32, (8, 128), 0)
    G = B // 8
    for blk in range(K // B):
        r0 = blk * B
        t0 = r0 // 128
        tiles = list(range(t0, 3))
        v = [[w[r0 + 8 * s:r0 + 8 * s + 8, t * 128:(t + 1) * 128] for t in tiles] for s in range(G)]
        scales = []
        for s0 in range(G):
            lane = (r0 + 8 * s0) % 128
            col = {
                s: [jnp.broadcast_to(v[s][0][:, lane + k:lane + k + 1], (8, 128)) for k in range(8)]
                for s in range(s0, G)
            }
            dvec = jnp.zeros((8, 128), F32)
            for j in range(8):
                prow = [jnp.broadcast_to(v[s0][t][j:j + 1], (8, 128)) for t in range(len(tiles))]
                pcol = [jnp.broadcast_to(col[s0][k][j:j + 1], (8, 128)) if k >= j else None
                        for k in range(8)]
                inv = 1.0 / pcol[j]
                dvec = jnp.where(sub == j, pcol[j], dvec)
                for s in range(s0, G):
                    mult = col[s][j] * inv
                    if s == s0:
                        mult = jnp.where(sub > j, mult, 0.0)
                    for k in range(j + 1, 8):
                        col[s][k] = col[s][k] - mult * pcol[k]
                    for t in range(len(tiles)):
                        v[s][t] = v[s][t] - mult * prow[t]
            scales.append(lax.rsqrt(dvec))
        for s in range(G):
            for t in range(len(tiles)):
                v[s][t] = v[s][t] * scales[s]
                if tiles[t] == 2:
                    w[r0 + 8 * s:r0 + 8 * s + 8, 256:384] = v[s][t]
        if blk + 1 < K // B:
            rows = jnp.concatenate([jnp.concatenate(v[s], axis=1) for s in range(G)], axis=0)
            h, m, l = split3(rows)
            n0 = ((r0 + B) // 128) * 128 - t0 * 128
            left = jnp.concatenate([h, h, m, m, h, l], axis=0)
            right = jnp.concatenate([h, m, h, m, l, h], axis=0)
            upd = lax.dot_general(left[:, n0:K - t0 * 128], right[:, n0:], (((0,), (0,)), ((), ())),
                                  preferred_element_type=F32)
            c0 = t0 * 128 + n0
            w[r0 + B:K, c0:384] = w[r0 + B:K, c0:384] - upd[r0 + B - c0:]
    out_ref[0] = w[:, 256:384].T[:own]


def factor(cfg, z, gram, block=32):
    def body(z_ref, gram_ref, out_ref, w):
        factor_kernel(1.0 / float(cfg.F), block, z_ref, gram_ref, out_ref, w)

    return pl.pallas_call(
        body,
        out_shape=jax.ShapeDtypeStruct((1, cfg.OWN, cfg.K), F32),
        in_specs=[pl.BlockSpec(memory_space=pltpu.VMEM)] * 2,
        out_specs=pl.BlockSpec(memory_space=pltpu.VMEM),
        scratch_shapes=[pltpu.VMEM((cfg.K, 384), F32)],
        compiler_params=pltpu.CompilerParams(vmem_limit_bytes=8 << 20),
        name="factor_rows",
    )(z, gram)


def solution(mesh):
    cfg = Cfg(zl=2, x=4, y=8, zh=4, core=2, tokens=512)

    def per_device(data, basis):
        z, gram = communicate(cfg, basis, data)
        return factor(cfg, z, gram)

    return jax.shard_map(
        per_device, mesh=mesh, in_specs=(P("dp", "feat"), P("feat", "dp", None)),
        out_specs=P("feat", "dp", None), check_vma=False,
    )
```

```python
import jax
import jax.numpy as jnp
from jax import lax
from jax.experimental import pallas as pl
from jax.experimental.pallas import tpu as pltpu
from jax.sharding import PartitionSpec as P

F32 = jnp.float32
BF16 = jnp.bfloat16
MESH = pl.DeviceIdType.MESH
HI = lax.Precision.HIGHEST


TURN = 0.1
LATER = 6


class Cfg:
    def __init__(self, zl, x, y, zh, core, tokens, own=56, width=256, alpha=80, chunks=1,
                 trees=("skip", "skip", "skip", "skip")):
        self.ZL, self.X, self.Y, self.ZH, self.C = zl, x, y, zh, core
        self.T, self.OWN, self.K = tokens, own, width
        self.Z = zl * zh
        self.NC, self.CW = chunks, width // chunks
        self.FE = zh * core
        self.DP = zl * x * y
        self.FS = own * self.DP
        self.TOTAL_T = tokens * self.DP
        self.F = self.FS * self.FE
        self.MX = x * core
        self.RX = width // self.MX
        self.RZ = self.RX * 2 // self.Z
        self.alpha = alpha
        self.beta = 2 * own - alpha
        self.trees = [tree(y, kind) for kind in trees]


def tree(n, kind):
    up, down = n // 2, n // 2 - 1
    out = {}
    for h in range(1, up + 1):
        for d in ([1, -1] if h <= down else [1]):
            out[d * h] = d * (0 if kind == "direct" or h <= 2 else 2)
    return out


def position(h, n):
    s = (h + n + n // 2 - 1) % n - (n // 2 - 1)
    up = (s + n // 2 - 1) // (n // 2)
    return 2 * s * (2 * up - 1) - up


def comm_kernel(cfg, basis_ref, data_hbm, z_ref, gram_ref,
                xb, bb, zs, zr, ga_all, gb_all, q_all, ypart_all, ysib_all, ypair_all, yr_all, yfull_all,
                zp_all, sax_all, rax_all, say_all, ray_all, sby_all,
                rby_all, sbx_all, rbx_all, fin_all, zx_s_all, zx_r_all, xt,
                g1, r1, s1, r2, s2, r3, s3, a2, gfull,
                xsem, bsem, zsem, gsem, y_sems, ssem, zx_sem,
                m1, m2, m3, m4, m5):
    X, Y, Z, ZL, ZH, C = cfg.X, cfg.Y, cfg.Z, cfg.ZL, cfg.ZH, cfg.C
    FS = cfg.FS
    OWN, A, NC, CW = cfg.OWN, cfg.alpha, cfg.NC, cfg.CW
    dp = lax.axis_index("dp")
    feat = lax.axis_index("feat")
    my = dp % Y
    mx = (dp // Y) % X
    zl = dp // (X * Y)
    mc = feat % C
    mz = (feat // C) * ZL + zl
    me = {"x": mx, "y": my}

    def dev(ox=0, oy=0, oz=0, oc=0):
        x = (mx + ox + X) % X
        y = (my + oy + Y) % Y
        z = (mz + oz + Z) % Z
        c = (mc + oc) % C
        return {"dp": ((z % ZL) * X + x) * Y + y, "feat": (z // ZL) * C + c}

    partner = dev(oz=1 - 2 * zl)

    def rdma(src, dst, ssem, rsem, device):
        return pltpu.make_async_remote_copy(
            src_ref=src, dst_ref=dst, send_sem=ssem, recv_sem=rsem,
            device_id=device, device_id_type=MESH,
        )

    load = pltpu.make_async_copy(data_hbm, xb, xsem)
    load.start()

    fetch = pltpu.make_async_copy(basis_ref, bb, bsem)
    fetch.start()
    xc = [(ox, oc) for ox in range(X) for oc in range(C) if (ox, oc) != (0, 0)]
    fe = [(oz, oc) for oz in range(0, Z, ZL) for oc in range(C) if (oz, oc) != (0, 0)]
    peers = {(0, 0, oz, oc) for oz, oc in fe}
    peers |= {(ox, 0, 0, oc) for ox, oc in xc}
    peers |= {(0, oy, 0, 0) for oy in range(1, Y)}
    peers |= {(0, 0, oz, 0) for oz in range(1, Z)}
    barrier = pltpu.get_barrier_semaphore()
    for peer in sorted(peers):
        pl.semaphore_signal(barrier, inc=1, device_id=dev(*peer), device_id_type=MESH)
    fetch.wait()
    own = bb[0].astype(BF16).astype(F32)
    zs[...] = jnp.concatenate([own, jnp.zeros((64 - OWN, cfg.K), F32)], axis=0).astype(BF16)
    pl.semaphore_wait(barrier, len(peers))

    swap = rdma(zs, zr, zsem.at[0], zsem.at[1], partner)
    swap.start()
    swap.wait_recv()
    other = zr[...].astype(F32)[:OWN]
    unit = jnp.concatenate(
        [jnp.where(zl == 0, own, other), jnp.where(zl == 0, other, own)], axis=0
    ).astype(BF16)
    pos = lambda h: position(h, Y)
    for c in range(NC):
        ga_all[c, mx, 0] = unit[:A, c * CW:(c + 1) * CW]
        gb_all[c, my, mx] = unit[A:, c * CW:(c + 1) * CW]
    pending = [swap]
    xo = list(range(1, X))
    ta, tb = cfg.trees[:2]
    order = sorted(ta, key=pos)
    cuts = [(0, 0), (1, 1), (2, 2), (3, 3), (4, Y)]
    groups = [[h for h in [0] + order if lo <= abs(h) <= hi] for lo, hi in cuts]
    groups = [h for h in groups if h]
    first = [n for n in range(1, len(groups)) if abs(groups[n][0]) <= 2]
    later = [n for n in range(1, len(groups)) if abs(groups[n][0]) > 2]
    far = [h for n in later for h in groups[n]]

    def below(t, h):
        return sorted([k for k, v in t.items() if v == h], key=lambda k: -abs(k))

    def send(src, dst, sems, i, device):
        cp = rdma(src, dst, sems.at[0, i], sems.at[1, i], device)
        cp.start()
        pending.append(cp)

    def arrived(dst, sems, i):
        rdma(dst, dst, sems.at[0, i], sems.at[1, i], partner).wait_recv()

    def flush():
        while pending:
            pending.pop().wait_send()

    def span(group):
        return pl.ds(pos(group[0]), len(group))

    def gather(c):
        ga, gb = ga_all.at[c], gb_all.at[c]
        ax, ay, bx, by = [gsem.at[c, i] for i in range(4)]

        for i, o in enumerate(xo):
            send(gb.at[my, mx], gb.at[my, mx], bx, i, dev(ox=o))

        def along_y_a(h):
            for k in below(ta, h):
                send(ga.at[mx, pos(h)], ga.at[mx, pos(k)], ay, pos(k), dev(oy=k - h))

        def along_x_a(n):
            part = ga.at[mx, span(groups[n])]
            for i, o in enumerate(xo):
                send(part, part, ax, n * X + i, dev(ox=o))

        def along_y_b(h):
            part = gb.at[(my - h + Y) % Y]
            for k in below(tb, h):
                send(part, part, by, pos(k), dev(oy=k - h))

        def wait_b(h):
            arrived(gb.at[(my - h + Y) % Y], by, pos(h))

        along_y_a(0)
        along_x_a(0)
        yield 3.5
        for i, o in enumerate(xo):
            arrived(gb.at[my, (mx - o + X) % X], bx, i)
        along_y_b(0)
        yield 4.5
        for n in first:
            for h in groups[n]:
                arrived(ga.at[mx, pos(h)], ay, pos(h))
                along_y_a(h)
            along_x_a(n)
        yield 8
        for n in first[::-1]:
            for h in groups[n]:
                wait_b(h)
                along_y_b(h)
        yield 8.5
        for n in later:
            for h in groups[n]:
                arrived(ga.at[mx, pos(h)], ay, pos(h))
            along_x_a(n)
        yield 12
        for h in far:
            wait_b(h)
        for n in range(len(groups)):
            for i, o in enumerate(xo):
                arrived(ga.at[(mx - o + X) % X, span(groups[n])], ax, n * X + i)

    def arrange(c):
        ga, gb, q = ga_all.at[c], gb_all.at[c], q_all.at[c]

        def pair(i, carry):
            ux = i // (Y // 2)
            uy = (i % (Y // 2)) * 2
            a, b = [
                jnp.concatenate([ga[ux, pos(my - v + Y)].astype(F32), gb[v, ux].astype(F32)], axis=0)
                for v in (uy, uy + 1)
            ]
            for zz in range(ZL):
                rows = jnp.concatenate(
                    [a[zz * OWN:(zz + 1) * OWN], b[zz * OWN:(zz + 1) * OWN]], axis=0
                ).astype(BF16)
                at = pl.multiple_of(((zz * X + ux) * Y + uy) * OWN, 2 * OWN)
                q[pl.ds(at, 2 * OWN)] = rows
            return carry
        lax.fori_loop(0, X * Y // 2, pair, 0)

    TS = cfg.T // cfg.FE

    def sum_y(c):
        ypart, ysib, ypair = ypart_all.at[c], ysib_all.at[c], ypair_all.at[c]
        yr, yfull, q, y_sem = yr_all.at[c], yfull_all.at[c], q_all.at[c], y_sems.at[c]
        part = jnp.dot(xb[...], q[...], preferred_element_type=F32).astype(BF16)
        for h in range(C):
            for k in range(ZH):
                lo = (h * ZH + k) * TS
                ypart[h, k] = part[lo:lo + TS]
        mh = mz // ZL
        for h in range(1, C):
            cp = rdma(ypart.at[(mc + h) % C], ysib, y_sem.at[0, 0], y_sem.at[1, 0],
                      dev(oc=h))
            cp.start()
            pending.append(cp)
            yield 15
            cp.wait_recv()
        pair = ypart[mc].astype(F32) + ysib[...].astype(F32)
        ypair[...] = pair.astype(BF16)
        zoff = list(range(ZL, Z, ZL))
        for i, oz in enumerate(zoff):
            to = (mz + oz) % Z // ZL
            cp = rdma(ypair.at[to], yr.at[i], y_sem.at[0, 1 + i], y_sem.at[1, 1 + i],
                      dev(oz=oz))
            cp.start()
            pending.append(cp)
        yield 20.5
        total = ypart[mc, mh].astype(F32) + ysib[mh].astype(F32)
        for i in range(len(zoff)):
            rdma(yr.at[i], yr.at[i], y_sem.at[0, 1 + i], y_sem.at[1, 1 + i],
                 partner).wait_recv()
            total = total + yr[i].astype(F32)
        yfull[mc, mh] = total.astype(BF16)
        slot = yfull.at[mc, mh]
        for i, oz in enumerate(zoff):
            cp = rdma(slot, slot, y_sem.at[2, 1 + i], y_sem.at[3, 1 + i], dev(oz=oz))
            cp.start()
            pending.append(cp)
        yield 26
        for i, oz in enumerate(zoff):
            slot = yfull.at[mc, (mz + Z - oz) % Z // ZL]
            rdma(slot, slot, y_sem.at[2, 1 + i], y_sem.at[3, 1 + i], partner).wait_recv()
        slot = yfull.at[mc]
        for h in range(1, C):
            cp = rdma(slot, slot, y_sem.at[2, 0], y_sem.at[3, 0], dev(oc=h))
            cp.start()
            pending.append(cp)
            yield 27.5
            slot = yfull.at[(mc + h) % C]
            rdma(slot, slot, y_sem.at[2, 0], y_sem.at[3, 0], dev(oc=h)).wait_recv()

    def product(c):
        y = yfull_all[c].reshape(cfg.T, CW)
        zp_all[c] = jnp.dot(xt[...], y, preferred_element_type=F32)

    def turn(n, of):
        size = FS // of
        xt[n * size:(n + 1) * size] = xb[:, n * size:(n + 1) * size].T

    def scatter(c):
        ta, tb = cfg.trees[2:]
        zp, fin, zx_s, zx_r = zp_all.at[c], fin_all.at[c], zx_s_all.at[c], zx_r_all.at[c]
        sax, rax, say, ray = sax_all.at[c], rax_all.at[c], say_all.at[c], ray_all.at[c]
        sby, rby, sbx, rbx = sby_all.at[c], rby_all.at[c], sbx_all.at[c], rbx_all.at[c]
        ax, ay, bx, by = [ssem.at[c, i] for i in range(4)]

        def rows_a(hx, hy):
            u = ((mx - hx + X) % X) * Y + (my - hy + Y) % Y
            at0 = pl.multiple_of(u * OWN, OWN)
            at1 = pl.multiple_of((X * Y + u) * OWN, OWN)
            return jnp.concatenate([zp[pl.ds(at0, OWN)], zp[pl.ds(at1, A - OWN)]], axis=0)

        def rows_b(hx, hy):
            u = ((mx - hx + X) % X) * Y + (my - hy + Y) % Y
            return zp[pl.ds(pl.multiple_of((X * Y + u) * OWN + (A - OWN), 8), cfg.beta)]

        def out_x_a(n):
            for i, o in enumerate(xo):
                for h in groups[n]:
                    sax[i, pos(h)] = rows_a(o, h).astype(BF16)
                part = span(groups[n])
                send(sax.at[i, part], rax.at[i, part], ax, n * X + i, dev(ox=-o))

        def out_y_b(h):
            for hx in range(X):
                v = rows_b(hx, h)
                for k in below(tb, h):
                    v = v + rby[pos(k), hx].astype(F32)
                sby[pos(h), hx] = v.astype(BF16)
            send(sby.at[pos(h)], rby.at[pos(h)], by, pos(h), dev(oy=tb[h] - h))

        def sum_a(h):
            v = rows_a(0, h)
            for i in range(len(xo)):
                v = v + rax[i, pos(h)].astype(F32)
            for k in below(ta, h):
                v = v + ray[pos(k)].astype(F32)
            return v

        def out_y_a(h):
            say[pos(h)] = sum_a(h).astype(BF16)
            send(say.at[pos(h)], ray.at[pos(h)], ay, pos(h), dev(oy=ta[h] - h))

        def wait_x_a(n):
            for i in range(len(xo)):
                arrived(rax.at[i, span(groups[n])], ax, n * X + i)

        def wait_y(buf, sems, t, h):
            for k in below(t, h):
                arrived(buf.at[pos(k)], sems, pos(k))

        for n in later:
            out_x_a(n)
        for h in far:
            out_y_b(h)
        for n in first[::-1]:
            out_x_a(n)
            for h in groups[n]:
                if not below(tb, h):
                    out_y_b(h)
        out_x_a(0)
        yield 34
        for n in first[::-1]:
            for h in groups[n]:
                if below(tb, h):
                    wait_y(rby, by, tb, h)
                    out_y_b(h)
        yield 35
        for n in later:
            wait_x_a(n)
        for h in far:
            out_y_a(h)
        yield 36
        for n in first[::-1]:
            wait_x_a(n)
            for h in groups[n]:
                if below(ta, h):
                    wait_y(ray, ay, ta, h)
                out_y_a(h)
        yield 38.5
        wait_y(rby, by, tb, 0)
        for i, o in enumerate([0] + xo):
            v = rows_b(o, 0)
            for k in below(tb, 0):
                v = v + rby[pos(k), o].astype(F32)
            if o == 0:
                last_b = v
            else:
                sbx[i - 1] = v.astype(BF16)
                send(sbx.at[i - 1], rbx.at[i - 1], bx, i - 1, dev(ox=-o))
        yield 41
        wait_x_a(0)
        wait_y(ray, ay, ta, 0)
        fin[pl.ds(0, A)] = sum_a(0)
        for i in range(len(xo)):
            arrived(rbx.at[i], bx, i)
            last_b = last_b + rbx[i].astype(F32)
        fin[pl.ds(A, cfg.beta)] = last_b
        lo = fin[pl.ds(0, OWN)]
        hi = fin[pl.ds(OWN, OWN)]
        zx_s[...] = jnp.where(zl == 0, hi, lo)
        cp = rdma(zx_s, zx_r, zx_sem.at[c, 0], zx_sem.at[c, 1], partner)
        cp.start()
        pending.append(cp)
        yield 45
        cp.wait_recv()
        z_ref[:, c * CW:(c + 1) * CW] = (
            (jnp.where(zl == 0, lo, hi) + zx_r[...]) / float(cfg.TOTAL_T)
        )

    def gram_sum(z):
        gl = lax.dot_general(z, z, (((0,), (0,)), ((), ())), precision=HI, preferred_element_type=F32)
        g1[0] = gl[:, :128]
        g1[1] = gl[:, 128:]
        RX, RZ = cfg.RX, cfg.RZ
        m = mc * X + mx

        def exchange(offs, sems, src, dst, wait):
            copies = []
            for i, off in enumerate(offs):
                cp = rdma(src(off), dst(i), sems.at[0, i], sems.at[1, i], dev(*off))
                cp.start()
                copies.append(cp)
            flush()
            for i, off in enumerate(offs):
                back = wait(i, off)
                rdma(back, back, sems.at[0, i], sems.at[1, i], dev(*off)).wait_recv()
            pending.extend(copies)

        xoff = [(ox, 0, 0, oc) for ox, oc in xc]
        zoff = [(0, 0, oz, 0) for oz in range(1, Z)]
        yoff = [(0, oy, 0, 0) for oy in range(1, Y)]

        def rows1(off):
            t = ((mc + off[3]) % C) * X + (mx + off[0] + X) % X
            return pl.ds(pl.multiple_of(t * RX, RX), RX)

        mine = pl.ds(pl.multiple_of(m * RX, RX), RX)
        exchange(xoff, m1, lambda off: g1.at[:, rows1(off)], lambda i: r1.at[i], lambda i, off: r1.at[i])
        total = g1[:, mine]
        for i in range(len(xoff)):
            total = total + r1[i]
        s1[...] = total

        def tile(z):
            return z % 2, pl.ds(pl.multiple_of((z // 2) * RZ, RZ), RZ)

        def tile_to(off):
            return tile((mz + off[2] + Z) % Z)

        exchange(zoff, m2, lambda off: s1.at[tile_to(off)], lambda i: r2.at[i], lambda i, off: r2.at[i])
        half, rows = tile(mz)
        total = s1[half, rows]
        for i in range(len(zoff)):
            total = total + r2[i]
        s2[...] = total
        exchange(yoff, m3, lambda off: s2, lambda i: r3.at[i], lambda i, off: r3.at[i])
        total = s2[...]
        for i in range(len(yoff)):
            total = total + r3[i]
        a2[half, rows] = total
        own_tile = a2.at[half, rows]
        exchange(zoff, m4, lambda off: own_tile, lambda i: own_tile,
                 lambda i, off: a2.at[tile((mz - off[2] + Z) % Z)])
        gfull[:, mine] = a2[...]
        near = [off for off in xoff if off[3] == 0]
        exchange(near, m5, lambda off: a2, lambda i: gfull.at[:, mine],
                 lambda i, off: gfull.at[:, rows1((-off[0], 0, 0, 0))])
        for h in range(1, C):
            def half(c):
                return gfull.at[:, pl.ds(pl.multiple_of(c % C * (X * RX), X * RX), X * RX)]
            cp = rdma(half(mc), half(mc), m5.at[0, len(near)], m5.at[1, len(near)], dev(oc=h))
            cp.start()
            pending.append(cp)
            rdma(half(mc + h), half(mc + h), m5.at[0, len(near)], m5.at[1, len(near)],
                 dev(oc=h)).wait_recv()
        gram_ref[...] = gfull[...]

    def chain(c):
        yield from gather(c)
        arrange(c)
        yield from sum_y(c)
        product(c)
        yield from scatter(c)

    def turns(of):
        load.wait()
        for n in range(of):
            yield TURN + 0.5 * n
            turn(n, of)

    running = [[0.0, c, chain(c)] for c in range(NC)] + [[TURN, NC, turns(4)]]
    while running:
        running.sort(key=lambda r: r[:2])
        step = running[0]
        try:
            step[0] = next(step[2]) + (LATER * step[1] if step[1] < NC else 0)
        except StopIteration:
            running.remove(step)
    gram_sum(z_ref[...])
    flush()


def communicate(cfg, basis, data, vmem=48 << 20):
    X, Y, Z, C, ZH = cfg.X, cfg.Y, cfg.Z, cfg.C, cfg.ZH
    K, OWN, T, FS, A, B = cfg.K, cfg.OWN, cfg.T, cfg.FS, cfg.alpha, cfg.beta
    TS, N, W = T // cfg.FE, cfg.NC, cfg.CW
    nx, nz, ny = cfg.MX - 1, Z - 1, Y - 1
    VM = pltpu.VMEM
    DMA = pltpu.SemaphoreType.DMA
    scratch = [
        VM((T, FS), BF16), VM((1, OWN, K), F32), VM((64, K), BF16), VM((64, K), BF16),
        VM((N, X, Y, A, W), BF16), VM((N, Y, X, B, W), BF16), VM((N, FS, W), BF16),
        VM((N, C, ZH, TS, W), BF16), VM((N, ZH, TS, W), BF16), VM((N, ZH, TS, W), BF16),
        VM((N, ZH, TS, W), BF16), VM((N, C, ZH, TS, W), BF16),
        VM((N, FS, W), F32), VM((N, X - 1, Y, A, W), BF16), VM((N, X - 1, Y, A, W), BF16),
        VM((N, Y, A, W), BF16), VM((N, Y, A, W), BF16),
        VM((N, Y, X, B, W), BF16), VM((N, Y, X, B, W), BF16),
        VM((N, X - 1, B, W), BF16), VM((N, X - 1, B, W), BF16),
        VM((N, 2 * OWN, W), F32), VM((N, OWN, W), F32), VM((N, OWN, W), F32), VM((FS, T), BF16),
        VM((2, K, 128), F32), VM((nx, 2, cfg.RX, 128), F32), VM((2, cfg.RX, 128), F32),
        VM((nz, cfg.RZ, 128), F32), VM((cfg.RZ, 128), F32), VM((ny, cfg.RZ, 128), F32),
        VM((cfg.RZ, 128), F32), VM((2, cfg.RX, 128), F32), VM((2, K, 128), F32),
        DMA, DMA, DMA((2,)), DMA((N, 4, 2, 5 * X)), DMA((N, 4, 1 + ZH)),
        DMA((N, 4, 2, 5 * X)), DMA((N, 2)),
        DMA((2, nx)), DMA((2, nz)), DMA((2, ny)), DMA((2, nz)), DMA((2, nx)),
    ]

    def body(*refs):
        comm_kernel(cfg, *refs)

    return pl.pallas_call(
        body,
        out_shape=(
            jax.ShapeDtypeStruct((OWN, K), F32),
            jax.ShapeDtypeStruct((2, K, 128), F32),
        ),
        in_specs=[pl.BlockSpec(memory_space=pltpu.HBM)] * 2,
        out_specs=(pl.BlockSpec(memory_space=pltpu.VMEM), pl.BlockSpec(memory_space=pltpu.VMEM)),
        scratch_shapes=scratch,
        compiler_params=pltpu.CompilerParams(
            collective_id=0, has_side_effects=True, vmem_limit_bytes=vmem
        ),
        name="power_step",
    )(
        pltpu.with_memory_space_constraint(basis, pltpu.HBM),
        pltpu.with_memory_space_constraint(data, pltpu.HBM),
    )


def split3(v):
    h = v.astype(BF16)
    r = v - h.astype(F32)
    m = r.astype(BF16)
    return h, m, (r - m.astype(F32)).astype(BF16)


def factor_kernel(scale, B, z_ref, gram_ref, out_ref, w):
    own, K = z_ref.shape
    w[:, 0:128] = gram_ref[0] * scale
    w[:, 128:256] = gram_ref[1] * scale
    w[:, 256:384] = jnp.concatenate([z_ref[...], jnp.zeros((128 - own, K), F32)], axis=0).T
    sub = lax.broadcasted_iota(jnp.int32, (8, 128), 0)
    G = B // 8
    for blk in range(K // B):
        r0 = blk * B
        t0 = r0 // 128
        tiles = list(range(t0, 3))
        v = [[w[r0 + 8 * s:r0 + 8 * s + 8, t * 128:(t + 1) * 128] for t in tiles] for s in range(G)]
        scales = []
        for s0 in range(G):
            lane = (r0 + 8 * s0) % 128
            col = {
                s: [jnp.broadcast_to(v[s][0][:, lane + k:lane + k + 1], (8, 128)) for k in range(8)]
                for s in range(s0, G)
            }
            dvec = jnp.zeros((8, 128), F32)
            for j in range(8):
                prow = [jnp.broadcast_to(v[s0][t][j:j + 1], (8, 128)) for t in range(len(tiles))]
                pcol = [jnp.broadcast_to(col[s0][k][j:j + 1], (8, 128)) if k >= j else None
                        for k in range(8)]
                inv = 1.0 / pcol[j]
                dvec = jnp.where(sub == j, pcol[j], dvec)
                for s in range(s0, G):
                    mult = col[s][j] * inv
                    if s == s0:
                        mult = jnp.where(sub > j, mult, 0.0)
                    for k in range(j + 1, 8):
                        col[s][k] = col[s][k] - mult * pcol[k]
                    for t in range(len(tiles)):
                        v[s][t] = v[s][t] - mult * prow[t]
            scales.append(lax.rsqrt(dvec))
        for s in range(G):
            for t in range(len(tiles)):
                v[s][t] = v[s][t] * scales[s]
                if tiles[t] == 2:
                    w[r0 + 8 * s:r0 + 8 * s + 8, 256:384] = v[s][t]
        if blk + 1 < K // B:
            rows = jnp.concatenate([jnp.concatenate(v[s], axis=1) for s in range(G)], axis=0)
            h, m, l = split3(rows)
            n0 = ((r0 + B) // 128) * 128 - t0 * 128
            left = jnp.concatenate([h, h, m, m, h, l], axis=0)
            right = jnp.concatenate([h, m, h, m, l, h], axis=0)
            upd = lax.dot_general(left[:, n0:K - t0 * 128], right[:, n0:], (((0,), (0,)), ((), ())),
                                  preferred_element_type=F32)
            c0 = t0 * 128 + n0
            w[r0 + B:K, c0:384] = w[r0 + B:K, c0:384] - upd[r0 + B - c0:]
    out_ref[0] = w[:, 256:384].T[:own]


def factor(cfg, z, gram, block=32):
    def body(z_ref, gram_ref, out_ref, w):
        factor_kernel(1.0 / float(cfg.F), block, z_ref, gram_ref, out_ref, w)

    return pl.pallas_call(
        body,
        out_shape=jax.ShapeDtypeStruct((1, cfg.OWN, cfg.K), F32),
        in_specs=[pl.BlockSpec(memory_space=pltpu.VMEM)] * 2,
        out_specs=pl.BlockSpec(memory_space=pltpu.VMEM),
        scratch_shapes=[pltpu.VMEM((cfg.K, 384), F32)],
        compiler_params=pltpu.CompilerParams(vmem_limit_bytes=8 << 20),
        name="factor_rows",
    )(z, gram)


def solution(mesh):
    cfg = Cfg(zl=2, x=4, y=8, zh=4, core=2, tokens=512)

    def per_device(data, basis):
        z, gram = communicate(cfg, basis, data)
        return factor(cfg, z, gram)

    return jax.shard_map(
        per_device, mesh=mesh, in_specs=(P("dp", "feat"), P("feat", "dp", None)),
        out_specs=P("feat", "dp", None), check_vma=False,
    )
```

```python
import jax
import jax.numpy as jnp
from jax import lax
from jax.experimental import pallas as pl
from jax.experimental.pallas import tpu as pltpu
from jax.sharding import PartitionSpec as P

F32 = jnp.float32
BF16 = jnp.bfloat16
MESH = pl.DeviceIdType.MESH
HI = lax.Precision.HIGHEST


TURN = 0.1
LATER = 6


class Cfg:
    def __init__(self, zl, x, y, zh, core, tokens, own=56, width=256, alpha=80, chunks=1,
                 trees=("skip", "skip", "skip", "skip")):
        self.ZL, self.X, self.Y, self.ZH, self.C = zl, x, y, zh, core
        self.T, self.OWN, self.K = tokens, own, width
        self.Z = zl * zh
        self.NC, self.CW = chunks, width // chunks
        self.FE = zh * core
        self.DP = zl * x * y
        self.FS = own * self.DP
        self.TOTAL_T = tokens * self.DP
        self.F = self.FS * self.FE
        self.MX = x * core
        self.RX = width // self.MX
        self.RZ = self.RX * 2 // self.Z
        self.alpha = alpha
        self.beta = 2 * own - alpha
        self.trees = [tree(y, kind) for kind in trees]


def tree(n, kind):
    up, down = n // 2, n // 2 - 1
    out = {}
    for h in range(1, up + 1):
        for d in ([1, -1] if h <= down else [1]):
            out[d * h] = d * (0 if kind == "direct" or h <= 2 else 2)
    return out


def position(h, n):
    s = (h + n + n // 2 - 1) % n - (n // 2 - 1)
    up = (s + n // 2 - 1) // (n // 2)
    return 2 * s * (2 * up - 1) - up


def comm_kernel(cfg, basis_ref, data_hbm, z_ref, gram_ref,
                xb, bb, zs, zr, ga_all, gb_all, q_all, ypart_all, ysib_all, ypair_all, yr_all, yfull_all,
                zp_all, sax_all, rax_all, say_all, ray_all, sby_all,
                rby_all, sbx_all, rbx_all, fin_all, zx_s_all, zx_r_all, xt,
                g1, r1, s1, r2, s2, r3, s3, a2, gfull,
                xsem, bsem, zsem, gsem, y_sems, ssem, zx_sem,
                m1, m2, m3, m4, m5, far_sem):
    X, Y, Z, ZL, ZH, C = cfg.X, cfg.Y, cfg.Z, cfg.ZL, cfg.ZH, cfg.C
    FS = cfg.FS
    OWN, A, NC, CW = cfg.OWN, cfg.alpha, cfg.NC, cfg.CW
    dp = lax.axis_index("dp")
    feat = lax.axis_index("feat")
    my = dp % Y
    mx = (dp // Y) % X
    zl = dp // (X * Y)
    mc = feat % C
    mz = (feat // C) * ZL + zl
    me = {"x": mx, "y": my}

    def dev(ox=0, oy=0, oz=0, oc=0):
        x = (mx + ox + X) % X
        y = (my + oy + Y) % Y
        z = (mz + oz + Z) % Z
        c = (mc + oc) % C
        return {"dp": ((z % ZL) * X + x) * Y + y, "feat": (z // ZL) * C + c}

    partner = dev(oz=1 - 2 * zl)

    def rdma(src, dst, ssem, rsem, device):
        return pltpu.make_async_remote_copy(
            src_ref=src, dst_ref=dst, send_sem=ssem, recv_sem=rsem,
            device_id=device, device_id_type=MESH,
        )

    load = pltpu.make_async_copy(data_hbm, xb, xsem)
    load.start()

    fetch = pltpu.make_async_copy(basis_ref, bb, bsem)
    fetch.start()
    xc = [(ox, oc) for ox in range(X) for oc in range(C) if (ox, oc) != (0, 0)]
    peers = {(o % X, 0, 0, 0) for o in range(1, X)}
    peers |= {(0, o % Y, 0, 0) for o in (1, 2, -1, -2)}
    peers |= {(0, 0, o % Z, 0) for o in (ZL, -ZL) if o % Z}
    peers |= {(0, 0, 0, oc) for oc in range(1, C)}
    barrier = pltpu.get_barrier_semaphore()
    pl.semaphore_signal(barrier, inc=1, device_id=partner, device_id_type=MESH)
    for peer in sorted(peers):
        pl.semaphore_signal(barrier, inc=1, device_id=dev(*peer), device_id_type=MESH)
    fetch.wait()
    own = bb[0].astype(BF16).astype(F32)
    zs[...] = jnp.concatenate([own, jnp.zeros((64 - OWN, cfg.K), F32)], axis=0).astype(BF16)
    pl.semaphore_wait(barrier, len(peers) + 1)

    swap = rdma(zs, zr, zsem.at[0], zsem.at[1], partner)
    swap.start()
    if ZH > 1:
        pl.semaphore_signal(far_sem, inc=1, device_id=dev(oz=ZL), device_id_type=MESH)
    swap.wait_recv()
    other = zr[...].astype(F32)[:OWN]
    unit = jnp.concatenate(
        [jnp.where(zl == 0, own, other), jnp.where(zl == 0, other, own)], axis=0
    ).astype(BF16)
    pos = lambda h: position(h, Y)
    for c in range(NC):
        ga_all[c, mx, 0] = unit[:A, c * CW:(c + 1) * CW]
        gb_all[c, my, mx] = unit[A:, c * CW:(c + 1) * CW]
    pending = [swap]
    ring = lambda n: sorted(range(1, n), key=lambda o: -min(o, n - o))
    xo = ring(X)
    ta, tb = cfg.trees[:2]
    order = sorted(ta, key=pos)
    cuts = [(0, 0), (1, 1), (2, 2), (3, 3), (4, Y)]
    groups = [[h for h in [0] + order if lo <= abs(h) <= hi] for lo, hi in cuts]
    groups = [h for h in groups if h]
    first = [n for n in range(1, len(groups)) if abs(groups[n][0]) <= 2]
    later = [n for n in range(1, len(groups)) if abs(groups[n][0]) > 2]
    far = [h for n in later for h in groups[n]]

    def below(t, h):
        return sorted([k for k, v in t.items() if v == h], key=lambda k: -abs(k))

    def send(src, dst, sems, i, device):
        cp = rdma(src, dst, sems.at[0, i], sems.at[1, i], device)
        cp.start()
        pending.append(cp)

    def arrived(dst, sems, i):
        rdma(dst, dst, sems.at[0, i], sems.at[1, i], partner).wait_recv()

    def flush():
        while pending:
            pending.pop().wait_send()

    def span(group):
        return pl.ds(pos(group[0]), len(group))

    def gather(c):
        ga, gb = ga_all.at[c], gb_all.at[c]
        ax, ay, bx, by = [gsem.at[c, i] for i in range(4)]

        for i, o in enumerate(xo):
            send(gb.at[my, mx], gb.at[my, mx], bx, i, dev(ox=o))

        def along_y_a(h):
            for k in below(ta, h):
                send(ga.at[mx, pos(h)], ga.at[mx, pos(k)], ay, pos(k), dev(oy=k - h))

        def along_x_a(n):
            part = ga.at[mx, span(groups[n])]
            for i, o in enumerate(xo):
                send(part, part, ax, n * X + i, dev(ox=o))

        def along_y_b(h):
            part = gb.at[(my - h + Y) % Y]
            for k in below(tb, h):
                send(part, part, by, pos(k), dev(oy=k - h))

        def wait_b(h):
            arrived(gb.at[(my - h + Y) % Y], by, pos(h))

        along_y_a(0)
        along_x_a(0)
        yield 3.5
        for i, o in enumerate(xo):
            arrived(gb.at[my, (mx - o + X) % X], bx, i)
        along_y_b(0)
        yield 4.5
        for n in first:
            for h in groups[n]:
                arrived(ga.at[mx, pos(h)], ay, pos(h))
                along_y_a(h)
            along_x_a(n)
        yield 8
        for n in first[::-1]:
            for h in groups[n]:
                wait_b(h)
                along_y_b(h)
        yield 8.5
        for n in later:
            for h in groups[n]:
                arrived(ga.at[mx, pos(h)], ay, pos(h))
            along_x_a(n)
        yield 12
        for h in far:
            wait_b(h)
        for n in range(len(groups)):
            for i, o in enumerate(xo):
                arrived(ga.at[(mx - o + X) % X, span(groups[n])], ax, n * X + i)

    def arrange(c):
        ga, gb, q = ga_all.at[c], gb_all.at[c], q_all.at[c]

        def pair(i, carry):
            ux = i // (Y // 2)
            uy = (i % (Y // 2)) * 2
            a, b = [
                jnp.concatenate([ga[ux, pos(my - v + Y)].astype(F32), gb[v, ux].astype(F32)], axis=0)
                for v in (uy, uy + 1)
            ]
            for zz in range(ZL):
                rows = jnp.concatenate(
                    [a[zz * OWN:(zz + 1) * OWN], b[zz * OWN:(zz + 1) * OWN]], axis=0
                ).astype(BF16)
                at = pl.multiple_of(((zz * X + ux) * Y + uy) * OWN, 2 * OWN)
                q[pl.ds(at, 2 * OWN)] = rows
            return carry
        lax.fori_loop(0, X * Y // 2, pair, 0)

    TS = cfg.T // cfg.FE

    def sum_y(c):
        ypart, ysib, ypair = ypart_all.at[c], ysib_all.at[c], ypair_all.at[c]
        yr, yfull, q, y_sem = yr_all.at[c], yfull_all.at[c], q_all.at[c], y_sems.at[c]
        part = jnp.dot(xb[...], q[...], preferred_element_type=F32).astype(BF16)
        for h in range(C):
            for k in range(ZH):
                lo = (h * ZH + k) * TS
                ypart[h, k] = part[lo:lo + TS]
        mh = mz // ZL
        for h in range(1, C):
            cp = rdma(ypart.at[(mc + h) % C], ysib, y_sem.at[0, 0], y_sem.at[1, 0],
                      dev(oc=h))
            cp.start()
            pending.append(cp)
            yield 15
            cp.wait_recv()
        pair = ypart[mc].astype(F32) + ysib[...].astype(F32)
        ypair[...] = pair.astype(BF16)
        zoff = [ZL * o for o in ring(ZH)]
        if zoff:
            pl.semaphore_wait(far_sem, 1)
        for i, oz in enumerate(zoff):
            to = (mz + oz) % Z // ZL
            cp = rdma(ypair.at[to], yr.at[i], y_sem.at[0, 1 + i], y_sem.at[1, 1 + i],
                      dev(oz=oz))
            cp.start()
            pending.append(cp)
        flush()
        yield 20.5
        total = ypart[mc, mh].astype(F32) + ysib[mh].astype(F32)
        for i in range(len(zoff)):
            rdma(yr.at[i], yr.at[i], y_sem.at[0, 1 + i], y_sem.at[1, 1 + i],
                 partner).wait_recv()
            total = total + yr[i].astype(F32)
        yfull[mc, mh] = total.astype(BF16)
        slot = yfull.at[mc, mh]
        for i, oz in enumerate(zoff):
            cp = rdma(slot, slot, y_sem.at[2, 1 + i], y_sem.at[3, 1 + i], dev(oz=oz))
            cp.start()
            pending.append(cp)
        yield 26
        for i, oz in enumerate(zoff):
            slot = yfull.at[mc, (mz + Z - oz) % Z // ZL]
            rdma(slot, slot, y_sem.at[2, 1 + i], y_sem.at[3, 1 + i], partner).wait_recv()
        slot = yfull.at[mc]
        for h in range(1, C):
            cp = rdma(slot, slot, y_sem.at[2, 0], y_sem.at[3, 0], dev(oc=h))
            cp.start()
            pending.append(cp)
            yield 27.5
            slot = yfull.at[(mc + h) % C]
            rdma(slot, slot, y_sem.at[2, 0], y_sem.at[3, 0], dev(oc=h)).wait_recv()

    def product(c):
        y = yfull_all[c].reshape(cfg.T, CW)
        tile = 2 * OWN * (4 if FS % (8 * OWN) == 0 else 1)

        def one(i, carry):
            rows = pl.ds(pl.multiple_of(i * tile, tile), tile)
            zp_all[c, rows] = jnp.dot(xt[rows], y, preferred_element_type=F32)
            return carry
        lax.fori_loop(0, FS // tile, one, 0)

    def turn(n, of):
        def one(i, carry):
            rows = pl.ds(pl.multiple_of(i * 128, 128), 128)
            xt[rows] = xb[:, rows].T
            return carry
        tiles = FS // 128
        lax.fori_loop(n * tiles // of, (n + 1) * tiles // of, one, 0)

    def scatter(c):
        ta, tb = cfg.trees[2:]
        zp, fin, zx_s, zx_r = zp_all.at[c], fin_all.at[c], zx_s_all.at[c], zx_r_all.at[c]
        sax, rax, say, ray = sax_all.at[c], rax_all.at[c], say_all.at[c], ray_all.at[c]
        sby, rby, sbx, rbx = sby_all.at[c], rby_all.at[c], sbx_all.at[c], rbx_all.at[c]
        ax, ay, bx, by = [ssem.at[c, i] for i in range(4)]

        def rows_a(hx, hy):
            u = ((mx - hx + X) % X) * Y + (my - hy + Y) % Y
            at0 = pl.multiple_of(u * OWN, OWN)
            at1 = pl.multiple_of((X * Y + u) * OWN, OWN)
            return jnp.concatenate([zp[pl.ds(at0, OWN)], zp[pl.ds(at1, A - OWN)]], axis=0)

        def rows_b(hx, hy):
            u = ((mx - hx + X) % X) * Y + (my - hy + Y) % Y
            return zp[pl.ds(pl.multiple_of((X * Y + u) * OWN + (A - OWN), 8), cfg.beta)]

        def out_x_a(n):
            for i, o in enumerate(xo):
                for h in groups[n]:
                    sax[i, pos(h)] = rows_a(o, h).astype(BF16)
                part = span(groups[n])
                send(sax.at[i, part], rax.at[i, part], ax, n * X + i, dev(ox=-o))

        def out_y_b(h):
            for hx in range(X):
                v = rows_b(hx, h)
                for k in below(tb, h):
                    v = v + rby[pos(k), hx].astype(F32)
                sby[pos(h), hx] = v.astype(BF16)
            send(sby.at[pos(h)], rby.at[pos(h)], by, pos(h), dev(oy=tb[h] - h))

        def sum_a(h):
            v = rows_a(0, h)
            for i in range(len(xo)):
                v = v + rax[i, pos(h)].astype(F32)
            for k in below(ta, h):
                v = v + ray[pos(k)].astype(F32)
            return v

        def out_y_a(h):
            say[pos(h)] = sum_a(h).astype(BF16)
            send(say.at[pos(h)], ray.at[pos(h)], ay, pos(h), dev(oy=ta[h] - h))

        def wait_x_a(n):
            for i in range(len(xo)):
                arrived(rax.at[i, span(groups[n])], ax, n * X + i)

        def wait_y(buf, sems, t, h):
            for k in below(t, h):
                arrived(buf.at[pos(k)], sems, pos(k))

        for n in later:
            out_x_a(n)
        for h in far:
            out_y_b(h)
        for n in first[::-1]:
            out_x_a(n)
            for h in groups[n]:
                if not below(tb, h):
                    out_y_b(h)
        out_x_a(0)
        yield 34
        for n in first[::-1]:
            for h in groups[n]:
                if below(tb, h):
                    wait_y(rby, by, tb, h)
                    out_y_b(h)
        yield 35
        for n in later:
            wait_x_a(n)
        for h in far:
            out_y_a(h)
        yield 36
        for n in first[::-1]:
            wait_x_a(n)
            for h in groups[n]:
                if below(ta, h):
                    wait_y(ray, ay, ta, h)
                out_y_a(h)
        yield 38.5
        wait_y(rby, by, tb, 0)
        for i, o in enumerate([0] + xo):
            v = rows_b(o, 0)
            for k in below(tb, 0):
                v = v + rby[pos(k), o].astype(F32)
            if o == 0:
                last_b = v
            else:
                sbx[i - 1] = v.astype(BF16)
                send(sbx.at[i - 1], rbx.at[i - 1], bx, i - 1, dev(ox=-o))
        yield 41
        wait_x_a(0)
        wait_y(ray, ay, ta, 0)
        fin[pl.ds(0, A)] = sum_a(0)
        for i in range(len(xo)):
            arrived(rbx.at[i], bx, i)
            last_b = last_b + rbx[i].astype(F32)
        fin[pl.ds(A, cfg.beta)] = last_b
        lo = fin[pl.ds(0, OWN)]
        hi = fin[pl.ds(OWN, OWN)]
        zx_s[...] = jnp.concatenate(
            [jnp.where(zl == 0, hi, lo), jnp.zeros((64 - OWN, CW), F32)], axis=0
        ).astype(BF16)
        cp = rdma(zx_s, zx_r, zx_sem.at[c, 0], zx_sem.at[c, 1], partner)
        cp.start()
        pending.append(cp)
        flush()
        yield 45
        cp.wait_recv()
        z_ref[:, c * CW:(c + 1) * CW] = (
            (jnp.where(zl == 0, lo, hi) + zx_r[...].astype(F32)[:OWN]) / float(cfg.TOTAL_T)
        )

    def gram_sum(z):
        gl = lax.dot_general(z, z, (((0,), (0,)), ((), ())), precision=HI, preferred_element_type=F32)
        g1[0] = gl[:, :128]
        g1[1] = gl[:, 128:]
        RX, RZ = cfg.RX, cfg.RZ
        m = mc * X + mx

        def exchange(offs, sems, src, dst, wait):
            copies = []
            for i, off in enumerate(offs):
                cp = rdma(src(off), dst(i), sems.at[0, i], sems.at[1, i], dev(*off))
                cp.start()
                copies.append(cp)
            flush()
            for i, off in reversed(list(enumerate(offs))):
                back = wait(i, off)
                rdma(back, back, sems.at[0, i], sems.at[1, i], dev(*off)).wait_recv()
            pending.extend(copies)

        xoff = [(ox, 0, 0, oc) for ox in xo + [0] for oc in range(C) if (ox, oc) != (0, 0)]
        zoff = [(0, 0, oz, 0) for oz in ring(Z)]
        yoff = [(0, oy, 0, 0) for oy in ring(Y)]

        def rows1(off):
            t = ((mc + off[3]) % C) * X + (mx + off[0] + X) % X
            return pl.ds(pl.multiple_of(t * RX, RX), RX)

        mine = pl.ds(pl.multiple_of(m * RX, RX), RX)
        exchange(xoff, m1, lambda off: g1.at[:, rows1(off)], lambda i: r1.at[i], lambda i, off: r1.at[i])
        total = g1[:, mine]
        for i in range(len(xoff)):
            total = total + r1[i]
        s1[...] = total

        def tile(z):
            return z % 2, pl.ds(pl.multiple_of((z // 2) * RZ, RZ), RZ)

        def tile_to(off):
            return tile((mz + off[2] + Z) % Z)

        exchange(zoff, m2, lambda off: s1.at[tile_to(off)], lambda i: r2.at[i], lambda i, off: r2.at[i])
        half, rows = tile(mz)
        total = s1[half, rows]
        for i in range(len(zoff)):
            total = total + r2[i]
        s2[...] = total
        exchange(yoff, m3, lambda off: s2, lambda i: r3.at[i], lambda i, off: r3.at[i])
        total = s2[...]
        for i in range(len(yoff)):
            total = total + r3[i]
        a2[half, rows] = total
        own_tile = a2.at[half, rows]
        exchange(zoff, m4, lambda off: own_tile, lambda i: own_tile,
                 lambda i, off: a2.at[tile((mz - off[2] + Z) % Z)])
        gfull[:, mine] = a2[...]
        near = [off for off in xoff if off[3] == 0]
        exchange(near, m5, lambda off: a2, lambda i: gfull.at[:, mine],
                 lambda i, off: gfull.at[:, rows1((-off[0], 0, 0, 0))])
        for h in range(1, C):
            def half(c):
                return gfull.at[:, pl.ds(pl.multiple_of(c % C * (X * RX), X * RX), X * RX)]
            cp = rdma(half(mc), half(mc), m5.at[0, len(near)], m5.at[1, len(near)], dev(oc=h))
            cp.start()
            pending.append(cp)
            rdma(half(mc + h), half(mc + h), m5.at[0, len(near)], m5.at[1, len(near)],
                 dev(oc=h)).wait_recv()
        gram_ref[...] = gfull[...]

    def chain(c):
        yield from gather(c)
        arrange(c)
        yield from sum_y(c)
        product(c)
        yield from scatter(c)

    def turns(of):
        load.wait()
        for n in range(of):
            yield TURN + 0.5 * n
            turn(n, of)

    running = [[0.0, c, chain(c)] for c in range(NC)] + [[TURN, NC, turns(4)]]
    while running:
        running.sort(key=lambda r: r[:2])
        step = running[0]
        try:
            step[0] = next(step[2]) + (LATER * step[1] if step[1] < NC else 0)
        except StopIteration:
            running.remove(step)
    gram_sum(z_ref[...])
    flush()


def communicate(cfg, basis, data, vmem=48 << 20):
    X, Y, Z, C, ZH = cfg.X, cfg.Y, cfg.Z, cfg.C, cfg.ZH
    K, OWN, T, FS, A, B = cfg.K, cfg.OWN, cfg.T, cfg.FS, cfg.alpha, cfg.beta
    TS, N, W = T // cfg.FE, cfg.NC, cfg.CW
    nx, nz, ny = cfg.MX - 1, Z - 1, Y - 1
    VM = pltpu.VMEM
    DMA = pltpu.SemaphoreType.DMA
    scratch = [
        VM((T, FS), BF16), VM((1, OWN, K), F32), VM((64, K), BF16), VM((64, K), BF16),
        VM((N, X, Y, A, W), BF16), VM((N, Y, X, B, W), BF16), VM((N, FS, W), BF16),
        VM((N, C, ZH, TS, W), BF16), VM((N, ZH, TS, W), BF16), VM((N, ZH, TS, W), BF16),
        VM((N, ZH, TS, W), BF16), VM((N, C, ZH, TS, W), BF16),
        VM((N, FS, W), F32), VM((N, X - 1, Y, A, W), BF16), VM((N, X - 1, Y, A, W), BF16),
        VM((N, Y, A, W), BF16), VM((N, Y, A, W), BF16),
        VM((N, Y, X, B, W), BF16), VM((N, Y, X, B, W), BF16),
        VM((N, X - 1, B, W), BF16), VM((N, X - 1, B, W), BF16),
        VM((N, 2 * OWN, W), F32), VM((N, 64, W), BF16), VM((N, 64, W), BF16), VM((FS, T), BF16),
        VM((2, K, 128), F32), VM((nx, 2, cfg.RX, 128), F32), VM((2, cfg.RX, 128), F32),
        VM((nz, cfg.RZ, 128), F32), VM((cfg.RZ, 128), F32), VM((ny, cfg.RZ, 128), F32),
        VM((cfg.RZ, 128), F32), VM((2, cfg.RX, 128), F32), VM((2, K, 128), F32),
        DMA, DMA, DMA((2,)), DMA((N, 4, 2, 5 * X)), DMA((N, 4, 1 + ZH)),
        DMA((N, 4, 2, 5 * X)), DMA((N, 2)),
        DMA((2, nx)), DMA((2, nz)), DMA((2, ny)), DMA((2, nz)), DMA((2, nx)),
        pltpu.SemaphoreType.REGULAR,
    ]

    def body(*refs):
        comm_kernel(cfg, *refs)

    return pl.pallas_call(
        body,
        out_shape=(
            jax.ShapeDtypeStruct((OWN, K), F32),
            jax.ShapeDtypeStruct((2, K, 128), F32),
        ),
        in_specs=[pl.BlockSpec(memory_space=pltpu.HBM)] * 2,
        out_specs=(pl.BlockSpec(memory_space=pltpu.VMEM), pl.BlockSpec(memory_space=pltpu.VMEM)),
        scratch_shapes=scratch,
        compiler_params=pltpu.CompilerParams(
            collective_id=0, has_side_effects=True, vmem_limit_bytes=vmem
        ),
        name="power_step",
    )(
        pltpu.with_memory_space_constraint(basis, pltpu.HBM),
        pltpu.with_memory_space_constraint(data, pltpu.HBM),
    )


def split3(v):
    h = v.astype(BF16)
    r = v - h.astype(F32)
    m = r.astype(BF16)
    return h, m, (r - m.astype(F32)).astype(BF16)


def factor_kernel(scale, B, z_ref, gram_ref, out_ref, w):
    own, K = z_ref.shape
    w[:, 0:128] = gram_ref[0] * scale
    w[:, 128:256] = gram_ref[1] * scale
    w[:, 256:384] = jnp.concatenate([z_ref[...], jnp.zeros((128 - own, K), F32)], axis=0).T
    sub = lax.broadcasted_iota(jnp.int32, (8, 128), 0)
    G = B // 8
    for blk in range(K // B):
        r0 = blk * B
        t0 = r0 // 128
        tiles = list(range(t0, 3))
        v = [[w[r0 + 8 * s:r0 + 8 * s + 8, t * 128:(t + 1) * 128] for t in tiles] for s in range(G)]
        scales = []
        for s0 in range(G):
            lane = (r0 + 8 * s0) % 128
            col = {
                s: [jnp.broadcast_to(v[s][0][:, lane + k:lane + k + 1], (8, 128)) for k in range(8)]
                for s in range(s0, G)
            }
            dvec = jnp.zeros((8, 128), F32)
            for j in range(8):
                prow = [jnp.broadcast_to(v[s0][t][j:j + 1], (8, 128)) for t in range(len(tiles))]
                pcol = [jnp.broadcast_to(col[s0][k][j:j + 1], (8, 128)) if k >= j else None
                        for k in range(8)]
                inv = 1.0 / pcol[j]
                dvec = jnp.where(sub == j, pcol[j], dvec)
                for s in range(s0, G):
                    mult = col[s][j] * inv
                    if s == s0:
                        mult = jnp.where(sub > j, mult, 0.0)
                    for k in range(j + 1, 8):
                        col[s][k] = col[s][k] - mult * pcol[k]
                    for t in range(len(tiles)):
                        v[s][t] = v[s][t] - mult * prow[t]
            scales.append(lax.rsqrt(dvec))
        for s in range(G):
            for t in range(len(tiles)):
                v[s][t] = v[s][t] * scales[s]
                if tiles[t] == 2:
                    w[r0 + 8 * s:r0 + 8 * s + 8, 256:384] = v[s][t]
        if blk + 1 < K // B:
            rows = jnp.concatenate([jnp.concatenate(v[s], axis=1) for s in range(G)], axis=0)
            h, m, l = split3(rows)
            n0 = ((r0 + B) // 128) * 128 - t0 * 128
            left = jnp.concatenate([h, h, m, m, h, l], axis=0)
            right = jnp.concatenate([h, m, h, m, l, h], axis=0)
            upd = lax.dot_general(left[:, n0:K - t0 * 128], right[:, n0:], (((0,), (0,)), ((), ())),
                                  preferred_element_type=F32)
            c0 = t0 * 128 + n0
            w[r0 + B:K, c0:384] = w[r0 + B:K, c0:384] - upd[r0 + B - c0:]
    out_ref[0] = w[:, 256:384].T[:own]


def factor(cfg, z, gram, block=32):
    def body(z_ref, gram_ref, out_ref, w):
        factor_kernel(1.0 / float(cfg.F), block, z_ref, gram_ref, out_ref, w)

    return pl.pallas_call(
        body,
        out_shape=jax.ShapeDtypeStruct((1, cfg.OWN, cfg.K), F32),
        in_specs=[pl.BlockSpec(memory_space=pltpu.VMEM)] * 2,
        out_specs=pl.BlockSpec(memory_space=pltpu.VMEM),
        scratch_shapes=[pltpu.VMEM((cfg.K, 384), F32)],
        compiler_params=pltpu.CompilerParams(vmem_limit_bytes=8 << 20),
        name="factor_rows",
    )(z, gram)


def solution(mesh):
    cfg = Cfg(zl=2, x=4, y=8, zh=4, core=2, tokens=512)

    def per_device(data, basis):
        z, gram = communicate(cfg, basis, data)
        return factor(cfg, z, gram)

    return jax.shard_map(
        per_device, mesh=mesh, in_specs=(P("dp", "feat"), P("feat", "dp", None)),
        out_specs=P("feat", "dp", None), check_vma=False,
    )
```

```python
import jax
import jax.numpy as jnp
from jax import lax
from jax.experimental import pallas as pl
from jax.experimental.pallas import tpu as pltpu
from jax.sharding import PartitionSpec as P

F32 = jnp.float32
BF16 = jnp.bfloat16
MESH = pl.DeviceIdType.MESH
HI = lax.Precision.HIGHEST


TURN = 0.1
LATER = 6


class Cfg:
    def __init__(self, zl, x, y, zh, core, tokens, own=56, width=256, alpha=80, chunks=1,
                 trees=("skip", "skip", "skip", "skip")):
        self.ZL, self.X, self.Y, self.ZH, self.C = zl, x, y, zh, core
        self.T, self.OWN, self.K = tokens, own, width
        self.Z = zl * zh
        self.NC, self.CW = chunks, width // chunks
        self.FE = zh * core
        self.DP = zl * x * y
        self.FS = own * self.DP
        self.TOTAL_T = tokens * self.DP
        self.F = self.FS * self.FE
        self.MX = x * core
        self.RX = width // self.MX
        self.RZ = self.RX * 2 // self.Z
        self.alpha = alpha
        self.beta = 2 * own - alpha
        self.trees = [tree(y, kind) for kind in trees]


def tree(n, kind):
    up, down = n // 2, n // 2 - 1
    out = {}
    for h in range(1, up + 1):
        for d in ([1, -1] if h <= down else [1]):
            out[d * h] = d * (0 if kind == "direct" or h <= 2 else 2)
    return out


def position(h, n):
    s = (h + n + n // 2 - 1) % n - (n // 2 - 1)
    up = (s + n // 2 - 1) // (n // 2)
    return 2 * s * (2 * up - 1) - up


def comm_kernel(cfg, basis_ref, data_hbm, z_ref, gram_ref,
                xb, bb, zs, zr, ga_all, gb_all, q_all, ypart_all, ysib_all, ypair_all, yr_all, yfull_all,
                zp_all, sax_all, rax_all, say_all, ray_all, sby_all,
                rby_all, sbx_all, rbx_all, fin_all, zx_s_all, zx_r_all, xt,
                g1, r1, s1, r2, s2, r3, s3, a2, gfull,
                xsem, bsem, zsem, gsem, y_sems, ssem, zx_sem,
                m1, m2, m3, m4, m5, far_sem):
    X, Y, Z, ZL, ZH, C = cfg.X, cfg.Y, cfg.Z, cfg.ZL, cfg.ZH, cfg.C
    FS = cfg.FS
    OWN, A, NC, CW = cfg.OWN, cfg.alpha, cfg.NC, cfg.CW
    dp = lax.axis_index("dp")
    feat = lax.axis_index("feat")
    my = dp % Y
    mx = (dp // Y) % X
    zl = dp // (X * Y)
    mc = feat % C
    mz = (feat // C) * ZL + zl
    me = {"x": mx, "y": my}

    def dev(ox=0, oy=0, oz=0, oc=0):
        x = (mx + ox + X) % X
        y = (my + oy + Y) % Y
        z = (mz + oz + Z) % Z
        c = (mc + oc) % C
        return {"dp": ((z % ZL) * X + x) * Y + y, "feat": (z // ZL) * C + c}

    partner = dev(oz=1 - 2 * zl)

    def rdma(src, dst, ssem, rsem, device):
        return pltpu.make_async_remote_copy(
            src_ref=src, dst_ref=dst, send_sem=ssem, recv_sem=rsem,
            device_id=device, device_id_type=MESH,
        )

    load = pltpu.make_async_copy(data_hbm, xb, xsem)
    load.start()

    fetch = pltpu.make_async_copy(basis_ref, bb, bsem)
    fetch.start()
    xc = [(ox, oc) for ox in range(X) for oc in range(C) if (ox, oc) != (0, 0)]
    peers = {(o % X, 0, 0, 0) for o in range(1, X)}
    peers |= {(0, o % Y, 0, 0) for o in (1, 2, -1, -2)}
    peers |= {(0, 0, o % Z, 0) for o in (ZL, -ZL) if o % Z}
    peers |= {(0, 0, 0, oc) for oc in range(1, C)}
    barrier = pltpu.get_barrier_semaphore()
    pl.semaphore_signal(barrier, inc=1, device_id=partner, device_id_type=MESH)
    for peer in sorted(peers):
        pl.semaphore_signal(barrier, inc=1, device_id=dev(*peer), device_id_type=MESH)
    fetch.wait()
    own = bb[0].astype(BF16).astype(F32)
    zs[...] = jnp.concatenate([own, jnp.zeros((64 - OWN, cfg.K), F32)], axis=0).astype(BF16)
    pl.semaphore_wait(barrier, len(peers) + 1)

    swap = rdma(zs, zr, zsem.at[0], zsem.at[1], partner)
    swap.start()
    if ZH > 1:
        pl.semaphore_signal(far_sem, inc=1, device_id=dev(oz=ZL), device_id_type=MESH)
    swap.wait_recv()
    other = zr[...].astype(F32)[:OWN]
    unit = jnp.concatenate(
        [jnp.where(zl == 0, own, other), jnp.where(zl == 0, other, own)], axis=0
    ).astype(BF16)
    pos = lambda h: position(h, Y)
    for c in range(NC):
        ga_all[c, mx, 0] = unit[:A, c * CW:(c + 1) * CW]
        gb_all[c, my, mx] = unit[A:, c * CW:(c + 1) * CW]
    pending = [swap]
    ring = lambda n: sorted(range(1, n), key=lambda o: -min(o, n - o))
    xo = ring(X)
    ta, tb = cfg.trees[:2]
    order = sorted(ta, key=pos)
    cuts = [(0, 0), (1, 1), (2, 2), (3, 3), (4, Y)]
    groups = [[h for h in [0] + order if lo <= abs(h) <= hi] for lo, hi in cuts]
    groups = [h for h in groups if h]
    first = [n for n in range(1, len(groups)) if abs(groups[n][0]) <= 2]
    later = [n for n in range(1, len(groups)) if abs(groups[n][0]) > 2]
    far = [h for n in later for h in groups[n]]

    def below(t, h):
        return sorted([k for k, v in t.items() if v == h], key=lambda k: -abs(k))

    def send(src, dst, sems, i, device):
        cp = rdma(src, dst, sems.at[0, i], sems.at[1, i], device)
        cp.start()
        pending.append(cp)

    def arrived(dst, sems, i):
        rdma(dst, dst, sems.at[0, i], sems.at[1, i], partner).wait_recv()

    def flush():
        while pending:
            pending.pop().wait_send()

    def span(group):
        return pl.ds(pos(group[0]), len(group))

    def gather(c):
        ga, gb = ga_all.at[c], gb_all.at[c]
        ax, ay, bx, by = [gsem.at[c, i] for i in range(4)]

        def along_y_a(h):
            for k in below(ta, h):
                send(ga.at[mx, pos(h)], ga.at[mx, pos(k)], ay, pos(k), dev(oy=k - h))

        def along_x_a(n):
            part = ga.at[mx, span(groups[n])]
            for i, o in enumerate(xo):
                if n in relayed and o == X // 2:
                    continue
                send(part, part, ax, n * X + i, dev(ox=o))

        relayed = [n for n in (0, 1) if X == 4 and n in [0] + first]
        went = set()

        def wait_x_a(n, o):
            if (n, o) not in went:
                arrived(ga.at[(mx - o + X) % X, span(groups[n])], ax, n * X + xo.index(o))
                went.add((n, o))

        def relay(n):
            o = 1 if n % 2 == 0 else X - 1
            wait_x_a(n, o)
            part = ga.at[(mx - o + X) % X, span(groups[n])]
            send(part, part, ax, n * X + xo.index(X // 2), dev(ox=o))

        def along_y_b(h):
            part = gb.at[(my - h + Y) % Y]
            for k in below(tb, h):
                send(part, part, by, pos(k), dev(oy=k - h))

        def wait_b(h):
            arrived(gb.at[(my - h + Y) % Y], by, pos(h))

        along_y_a(0)
        for i, o in enumerate(xo):
            send(gb.at[my, mx], gb.at[my, mx], bx, i, dev(ox=o))
        along_x_a(0)
        yield 3.5
        for i, o in enumerate(xo):
            arrived(gb.at[my, (mx - o + X) % X], bx, i)
        along_y_b(0)
        yield 4.5
        for n in first:
            for h in groups[n]:
                arrived(ga.at[mx, pos(h)], ay, pos(h))
                along_y_a(h)
            along_x_a(n)
        yield 8
        for n in first[::-1]:
            for h in groups[n]:
                wait_b(h)
                along_y_b(h)
        for n in relayed:
            relay(n)
        yield 8.5
        for n in later:
            for h in groups[n]:
                arrived(ga.at[mx, pos(h)], ay, pos(h))
            along_x_a(n)
        yield 12
        for h in far:
            wait_b(h)
        for n in range(len(groups)):
            for o in xo:
                wait_x_a(n, o)

    def arrange(c):
        ga, gb, q = ga_all.at[c], gb_all.at[c], q_all.at[c]

        def pair(i, carry):
            ux = i // (Y // 2)
            uy = (i % (Y // 2)) * 2
            a, b = [
                jnp.concatenate([ga[ux, pos(my - v + Y)].astype(F32), gb[v, ux].astype(F32)], axis=0)
                for v in (uy, uy + 1)
            ]
            for zz in range(ZL):
                rows = jnp.concatenate(
                    [a[zz * OWN:(zz + 1) * OWN], b[zz * OWN:(zz + 1) * OWN]], axis=0
                ).astype(BF16)
                at = pl.multiple_of(((zz * X + ux) * Y + uy) * OWN, 2 * OWN)
                q[pl.ds(at, 2 * OWN)] = rows
            return carry
        lax.fori_loop(0, X * Y // 2, pair, 0)

    TS = cfg.T // cfg.FE

    def sum_y(c):
        ypart, ysib, ypair = ypart_all.at[c], ysib_all.at[c], ypair_all.at[c]
        yr, yfull, q, y_sem = yr_all.at[c], yfull_all.at[c], q_all.at[c], y_sems.at[c]
        part = jnp.dot(xb[...], q[...], preferred_element_type=F32).astype(BF16)
        for h in range(C):
            for k in range(ZH):
                lo = (h * ZH + k) * TS
                ypart[h, k] = part[lo:lo + TS]
        mh = mz // ZL
        for h in range(1, C):
            cp = rdma(ypart.at[(mc + h) % C], ysib, y_sem.at[0, 0], y_sem.at[1, 0],
                      dev(oc=h))
            cp.start()
            pending.append(cp)
            yield 15
            cp.wait_recv()
        pair = ypart[mc].astype(F32) + ysib[...].astype(F32)
        ypair[...] = pair.astype(BF16)
        zoff = [ZL * o for o in ring(ZH)]
        if zoff:
            pl.semaphore_wait(far_sem, 1)
        for i, oz in enumerate(zoff):
            to = (mz + oz) % Z // ZL
            cp = rdma(ypair.at[to], yr.at[i], y_sem.at[0, 1 + i], y_sem.at[1, 1 + i],
                      dev(oz=oz))
            cp.start()
            pending.append(cp)
        flush()
        yield 20.5
        total = ypart[mc, mh].astype(F32) + ysib[mh].astype(F32)
        for i in range(len(zoff)):
            rdma(yr.at[i], yr.at[i], y_sem.at[0, 1 + i], y_sem.at[1, 1 + i],
                 partner).wait_recv()
            total = total + yr[i].astype(F32)
        yfull[mc, mh] = total.astype(BF16)
        slot = yfull.at[mc, mh]
        for i, oz in enumerate(zoff):
            cp = rdma(slot, slot, y_sem.at[2, 1 + i], y_sem.at[3, 1 + i], dev(oz=oz))
            cp.start()
            pending.append(cp)
        yield 26
        for i, oz in enumerate(zoff):
            slot = yfull.at[mc, (mz + Z - oz) % Z // ZL]
            rdma(slot, slot, y_sem.at[2, 1 + i], y_sem.at[3, 1 + i], partner).wait_recv()
        slot = yfull.at[mc]
        for h in range(1, C):
            cp = rdma(slot, slot, y_sem.at[2, 0], y_sem.at[3, 0], dev(oc=h))
            cp.start()
            pending.append(cp)
            yield 27.5
            slot = yfull.at[(mc + h) % C]
            rdma(slot, slot, y_sem.at[2, 0], y_sem.at[3, 0], dev(oc=h)).wait_recv()

    def product(c):
        y = yfull_all[c].reshape(cfg.T, CW)
        tile = 2 * OWN * (4 if FS % (8 * OWN) == 0 else 1)

        def one(i, carry):
            rows = pl.ds(pl.multiple_of(i * tile, tile), tile)
            zp_all[c, rows] = jnp.dot(xt[rows], y, preferred_element_type=F32)
            return carry
        lax.fori_loop(0, FS // tile, one, 0)

    def turn(n, of):
        def one(i, carry):
            rows = pl.ds(pl.multiple_of(i * 128, 128), 128)
            xt[rows] = xb[:, rows].T
            return carry
        tiles = FS // 128
        lax.fori_loop(n * tiles // of, (n + 1) * tiles // of, one, 0)

    def scatter(c):
        ta, tb = cfg.trees[2:]
        zp, fin, zx_s, zx_r = zp_all.at[c], fin_all.at[c], zx_s_all.at[c], zx_r_all.at[c]
        sax, rax, say, ray = sax_all.at[c], rax_all.at[c], say_all.at[c], ray_all.at[c]
        sby, rby, sbx, rbx = sby_all.at[c], rby_all.at[c], sbx_all.at[c], rbx_all.at[c]
        ax, ay, bx, by = [ssem.at[c, i] for i in range(4)]

        def rows_a(hx, hy):
            u = ((mx - hx + X) % X) * Y + (my - hy + Y) % Y
            at0 = pl.multiple_of(u * OWN, OWN)
            at1 = pl.multiple_of((X * Y + u) * OWN, OWN)
            return jnp.concatenate([zp[pl.ds(at0, OWN)], zp[pl.ds(at1, A - OWN)]], axis=0)

        def rows_b(hx, hy):
            u = ((mx - hx + X) % X) * Y + (my - hy + Y) % Y
            return zp[pl.ds(pl.multiple_of((X * Y + u) * OWN + (A - OWN), 8), cfg.beta)]

        def out_x_a(n):
            for i, o in enumerate(xo):
                for h in groups[n]:
                    sax[i, pos(h)] = rows_a(o, h).astype(BF16)
                part = span(groups[n])
                send(sax.at[i, part], rax.at[i, part], ax, n * X + i, dev(ox=-o))

        def out_y_b(h):
            for hx in range(X):
                v = rows_b(hx, h)
                for k in below(tb, h):
                    v = v + rby[pos(k), hx].astype(F32)
                sby[pos(h), hx] = v.astype(BF16)
            send(sby.at[pos(h)], rby.at[pos(h)], by, pos(h), dev(oy=tb[h] - h))

        def sum_a(h):
            v = rows_a(0, h)
            for i in range(len(xo)):
                v = v + rax[i, pos(h)].astype(F32)
            for k in below(ta, h):
                v = v + ray[pos(k)].astype(F32)
            return v

        def out_y_a(h):
            say[pos(h)] = sum_a(h).astype(BF16)
            send(say.at[pos(h)], ray.at[pos(h)], ay, pos(h), dev(oy=ta[h] - h))

        def wait_x_a(n):
            for i in range(len(xo)):
                arrived(rax.at[i, span(groups[n])], ax, n * X + i)

        def wait_y(buf, sems, t, h):
            for k in below(t, h):
                arrived(buf.at[pos(k)], sems, pos(k))

        for n in later:
            out_x_a(n)
        for h in far:
            out_y_b(h)
        for n in first[::-1]:
            out_x_a(n)
            for h in groups[n]:
                if not below(tb, h):
                    out_y_b(h)
        out_x_a(0)
        yield 34
        for n in first[::-1]:
            for h in groups[n]:
                if below(tb, h):
                    wait_y(rby, by, tb, h)
                    out_y_b(h)
        yield 35
        for n in later:
            wait_x_a(n)
        for h in far:
            out_y_a(h)
        yield 36
        for n in first[::-1]:
            wait_x_a(n)
            for h in groups[n]:
                if below(ta, h):
                    wait_y(ray, ay, ta, h)
                out_y_a(h)
        yield 38.5
        wait_y(rby, by, tb, 0)
        for i, o in enumerate([0] + xo):
            v = rows_b(o, 0)
            for k in below(tb, 0):
                v = v + rby[pos(k), o].astype(F32)
            if o == 0:
                last_b = v
            else:
                sbx[i - 1] = v.astype(BF16)
                send(sbx.at[i - 1], rbx.at[i - 1], bx, i - 1, dev(ox=-o))
        yield 41
        wait_x_a(0)
        wait_y(ray, ay, ta, 0)
        fin[pl.ds(0, A)] = sum_a(0)
        for i in range(len(xo)):
            arrived(rbx.at[i], bx, i)
            last_b = last_b + rbx[i].astype(F32)
        fin[pl.ds(A, cfg.beta)] = last_b
        lo = fin[pl.ds(0, OWN)]
        hi = fin[pl.ds(OWN, OWN)]
        zx_s[...] = jnp.concatenate(
            [jnp.where(zl == 0, hi, lo), jnp.zeros((64 - OWN, CW), F32)], axis=0
        ).astype(BF16)
        cp = rdma(zx_s, zx_r, zx_sem.at[c, 0], zx_sem.at[c, 1], partner)
        cp.start()
        pending.append(cp)
        flush()
        yield 45
        cp.wait_recv()
        z_ref[:, c * CW:(c + 1) * CW] = (
            (jnp.where(zl == 0, lo, hi) + zx_r[...].astype(F32)[:OWN]) / float(cfg.TOTAL_T)
        )

    def gram_sum(z):
        h, m, l = split3(jnp.concatenate([z, jnp.zeros((64 - OWN, cfg.K), F32)], axis=0))
        gl = lax.dot_general(
            jnp.concatenate([h, h, m, m, h, l], axis=0), jnp.concatenate([h, m, h, m, l, h], axis=0),
            (((0,), (0,)), ((), ())), preferred_element_type=F32,
        )
        g1[0] = gl[:, :128]
        g1[1] = gl[:, 128:]
        RX, RZ = cfg.RX, cfg.RZ
        m = mc * X + mx

        def exchange(offs, sems, src, dst, wait):
            copies = []
            for i, off in enumerate(offs):
                cp = rdma(src(off), dst(i), sems.at[0, i], sems.at[1, i], dev(*off))
                cp.start()
                copies.append(cp)
            flush()
            for i, off in reversed(list(enumerate(offs))):
                back = wait(i, off)
                rdma(back, back, sems.at[0, i], sems.at[1, i], dev(*off)).wait_recv()
            pending.extend(copies)

        xoff = [(ox, 0, 0, oc) for ox in xo + [0] for oc in range(C) if (ox, oc) != (0, 0)]
        zoff = [(0, 0, oz, 0) for oz in ring(Z)]
        yoff = [(0, oy, 0, 0) for oy in ring(Y)]

        def rows1(off):
            t = ((mc + off[3]) % C) * X + (mx + off[0] + X) % X
            return pl.ds(pl.multiple_of(t * RX, RX), RX)

        mine = pl.ds(pl.multiple_of(m * RX, RX), RX)
        exchange(xoff, m1, lambda off: g1.at[:, rows1(off)], lambda i: r1.at[i], lambda i, off: r1.at[i])
        total = g1[:, mine]
        for i in range(len(xoff)):
            total = total + r1[i]
        s1[...] = total

        def tile(z):
            return z % 2, pl.ds(pl.multiple_of((z // 2) * RZ, RZ), RZ)

        def tile_to(off):
            return tile((mz + off[2] + Z) % Z)

        exchange(zoff, m2, lambda off: s1.at[tile_to(off)], lambda i: r2.at[i], lambda i, off: r2.at[i])
        half, rows = tile(mz)
        total = s1[half, rows]
        for i in range(len(zoff)):
            total = total + r2[i]
        s2[...] = total
        exchange(yoff, m3, lambda off: s2, lambda i: r3.at[i], lambda i, off: r3.at[i])
        total = s2[...]
        for i in range(len(yoff)):
            total = total + r3[i]
        a2[half, rows] = total
        own_tile = a2.at[half, rows]
        exchange(zoff, m4, lambda off: own_tile, lambda i: own_tile,
                 lambda i, off: a2.at[tile((mz - off[2] + Z) % Z)])
        gfull[:, mine] = a2[...]
        near = [off for off in xoff if off[3] == 0]
        exchange(near, m5, lambda off: a2, lambda i: gfull.at[:, mine],
                 lambda i, off: gfull.at[:, rows1((-off[0], 0, 0, 0))])
        for h in range(1, C):
            def half(c):
                return gfull.at[:, pl.ds(pl.multiple_of(c % C * (X * RX), X * RX), X * RX)]
            cp = rdma(half(mc), half(mc), m5.at[0, len(near)], m5.at[1, len(near)], dev(oc=h))
            cp.start()
            pending.append(cp)
            rdma(half(mc + h), half(mc + h), m5.at[0, len(near)], m5.at[1, len(near)],
                 dev(oc=h)).wait_recv()
        gram_ref[...] = gfull[...]

    def chain(c):
        yield from gather(c)
        arrange(c)
        yield from sum_y(c)
        product(c)
        yield from scatter(c)

    def turns(of):
        load.wait()
        for n in range(of):
            yield TURN + 0.5 * n
            turn(n, of)

    running = [[0.0, c, chain(c)] for c in range(NC)] + [[TURN, NC, turns(4)]]
    while running:
        running.sort(key=lambda r: r[:2])
        step = running[0]
        try:
            step[0] = next(step[2]) + (LATER * step[1] if step[1] < NC else 0)
        except StopIteration:
            running.remove(step)
    gram_sum(z_ref[...])
    flush()


def communicate(cfg, basis, data, vmem=48 << 20):
    X, Y, Z, C, ZH = cfg.X, cfg.Y, cfg.Z, cfg.C, cfg.ZH
    K, OWN, T, FS, A, B = cfg.K, cfg.OWN, cfg.T, cfg.FS, cfg.alpha, cfg.beta
    TS, N, W = T // cfg.FE, cfg.NC, cfg.CW
    nx, nz, ny = cfg.MX - 1, Z - 1, Y - 1
    VM = pltpu.VMEM
    DMA = pltpu.SemaphoreType.DMA
    scratch = [
        VM((T, FS), BF16), VM((1, OWN, K), F32), VM((64, K), BF16), VM((64, K), BF16),
        VM((N, X, Y, A, W), BF16), VM((N, Y, X, B, W), BF16), VM((N, FS, W), BF16),
        VM((N, C, ZH, TS, W), BF16), VM((N, ZH, TS, W), BF16), VM((N, ZH, TS, W), BF16),
        VM((N, ZH, TS, W), BF16), VM((N, C, ZH, TS, W), BF16),
        VM((N, FS, W), F32), VM((N, X - 1, Y, A, W), BF16), VM((N, X - 1, Y, A, W), BF16),
        VM((N, Y, A, W), BF16), VM((N, Y, A, W), BF16),
        VM((N, Y, X, B, W), BF16), VM((N, Y, X, B, W), BF16),
        VM((N, X - 1, B, W), BF16), VM((N, X - 1, B, W), BF16),
        VM((N, 2 * OWN, W), F32), VM((N, 64, W), BF16), VM((N, 64, W), BF16), VM((FS, T), BF16),
        VM((2, K, 128), F32), VM((nx, 2, cfg.RX, 128), F32), VM((2, cfg.RX, 128), F32),
        VM((nz, cfg.RZ, 128), F32), VM((cfg.RZ, 128), F32), VM((ny, cfg.RZ, 128), F32),
        VM((cfg.RZ, 128), F32), VM((2, cfg.RX, 128), F32), VM((2, K, 128), F32),
        DMA, DMA, DMA((2,)), DMA((N, 4, 2, 5 * X)), DMA((N, 4, 1 + ZH)),
        DMA((N, 4, 2, 5 * X)), DMA((N, 2)),
        DMA((2, nx)), DMA((2, nz)), DMA((2, ny)), DMA((2, nz)), DMA((2, nx)),
        pltpu.SemaphoreType.REGULAR,
    ]

    def body(*refs):
        comm_kernel(cfg, *refs)

    return pl.pallas_call(
        body,
        out_shape=(
            jax.ShapeDtypeStruct((OWN, K), F32),
            jax.ShapeDtypeStruct((2, K, 128), F32),
        ),
        in_specs=[pl.BlockSpec(memory_space=pltpu.HBM)] * 2,
        out_specs=(pl.BlockSpec(memory_space=pltpu.VMEM), pl.BlockSpec(memory_space=pltpu.VMEM)),
        scratch_shapes=scratch,
        compiler_params=pltpu.CompilerParams(
            collective_id=0, has_side_effects=True, vmem_limit_bytes=vmem
        ),
        name="power_step",
    )(
        pltpu.with_memory_space_constraint(basis, pltpu.HBM),
        pltpu.with_memory_space_constraint(data, pltpu.HBM),
    )


def split3(v):
    h = v.astype(BF16)
    r = v - h.astype(F32)
    m = r.astype(BF16)
    return h, m, (r - m.astype(F32)).astype(BF16)


def factor_kernel(scale, B, z_ref, gram_ref, out_ref, w):
    own, K = z_ref.shape
    w[:, 0:128] = gram_ref[0] * scale
    w[:, 128:256] = gram_ref[1] * scale
    w[:, 256:384] = jnp.concatenate([z_ref[...], jnp.zeros((128 - own, K), F32)], axis=0).T
    sub = lax.broadcasted_iota(jnp.int32, (8, 128), 0)
    G = B // 8
    for blk in range(K // B):
        r0 = blk * B
        t0 = r0 // 128
        tiles = list(range(t0, 3))
        v = [[w[r0 + 8 * s:r0 + 8 * s + 8, t * 128:(t + 1) * 128] for t in tiles] for s in range(G)]
        scales = []
        for s0 in range(G):
            lane = (r0 + 8 * s0) % 128
            col = {
                s: [jnp.broadcast_to(v[s][0][:, lane + k:lane + k + 1], (8, 128)) for k in range(8)]
                for s in range(s0, G)
            }
            dvec = jnp.zeros((8, 128), F32)
            for j in range(8):
                prow = [jnp.broadcast_to(v[s0][t][j:j + 1], (8, 128)) for t in range(len(tiles))]
                pcol = [jnp.broadcast_to(col[s0][k][j:j + 1], (8, 128)) if k >= j else None
                        for k in range(8)]
                inv = 1.0 / pcol[j]
                dvec = jnp.where(sub == j, pcol[j], dvec)
                for s in range(s0, G):
                    mult = col[s][j] * inv
                    if s == s0:
                        mult = jnp.where(sub > j, mult, 0.0)
                    for k in range(j + 1, 8):
                        col[s][k] = col[s][k] - mult * pcol[k]
                    for t in range(len(tiles)):
                        v[s][t] = v[s][t] - mult * prow[t]
            scales.append(lax.rsqrt(dvec))
        for s in range(G):
            for t in range(len(tiles)):
                v[s][t] = v[s][t] * scales[s]
                if tiles[t] == 2:
                    w[r0 + 8 * s:r0 + 8 * s + 8, 256:384] = v[s][t]
        if blk + 1 < K // B:
            rows = jnp.concatenate([jnp.concatenate(v[s], axis=1) for s in range(G)], axis=0)
            h, m, l = split3(rows)
            n0 = ((r0 + B) // 128) * 128 - t0 * 128
            left = jnp.concatenate([h, h, m, m, h, l], axis=0)
            right = jnp.concatenate([h, m, h, m, l, h], axis=0)
            upd = lax.dot_general(left[:, n0:K - t0 * 128], right[:, n0:], (((0,), (0,)), ((), ())),
                                  preferred_element_type=F32)
            c0 = t0 * 128 + n0
            w[r0 + B:K, c0:384] = w[r0 + B:K, c0:384] - upd[r0 + B - c0:]
    out_ref[0] = w[:, 256:384].T[:own]


def factor(cfg, z, gram, block=32):
    def body(z_ref, gram_ref, out_ref, w):
        factor_kernel(1.0 / float(cfg.F), block, z_ref, gram_ref, out_ref, w)

    return pl.pallas_call(
        body,
        out_shape=jax.ShapeDtypeStruct((1, cfg.OWN, cfg.K), F32),
        in_specs=[pl.BlockSpec(memory_space=pltpu.VMEM)] * 2,
        out_specs=pl.BlockSpec(memory_space=pltpu.VMEM),
        scratch_shapes=[pltpu.VMEM((cfg.K, 384), F32)],
        compiler_params=pltpu.CompilerParams(vmem_limit_bytes=8 << 20),
        name="factor_rows",
    )(z, gram)


def solution(mesh):
    cfg = Cfg(zl=2, x=4, y=8, zh=4, core=2, tokens=512)

    def per_device(data, basis):
        z, gram = communicate(cfg, basis, data)
        return factor(cfg, z, gram)

    return jax.shard_map(
        per_device, mesh=mesh, in_specs=(P("dp", "feat"), P("feat", "dp", None)),
        out_specs=P("feat", "dp", None), check_vma=False,
    )
```

```python
import jax
import jax.numpy as jnp
from jax import lax
from jax.experimental import pallas as pl
from jax.experimental.pallas import tpu as pltpu
from jax.sharding import PartitionSpec as P

F32 = jnp.float32
BF16 = jnp.bfloat16
MESH = pl.DeviceIdType.MESH
HI = lax.Precision.HIGHEST


TURN = 0.1
LATER = 6


class Cfg:
    def __init__(self, zl, x, y, zh, core, tokens, own=56, width=256, alpha=80, chunks=1,
                 trees=("skip", "skip", "direct", "skip")):
        self.ZL, self.X, self.Y, self.ZH, self.C = zl, x, y, zh, core
        self.T, self.OWN, self.K = tokens, own, width
        self.Z = zl * zh
        self.NC, self.CW = chunks, width // chunks
        self.FE = zh * core
        self.DP = zl * x * y
        self.FS = own * self.DP
        self.TOTAL_T = tokens * self.DP
        self.F = self.FS * self.FE
        self.MX = x * core
        self.RX = width // self.MX
        self.RZ = self.RX * 2 // self.Z
        self.alpha = alpha
        self.beta = 2 * own - alpha
        self.trees = [tree(y, kind) for kind in trees]


def tree(n, kind):
    up, down = n // 2, n // 2 - 1
    out = {}
    for h in range(1, up + 1):
        for d in ([1, -1] if h <= down else [1]):
            out[d * h] = d * (0 if kind == "direct" or h <= 2 else 2)
    return out


def position(h, n):
    s = (h + n + n // 2 - 1) % n - (n // 2 - 1)
    up = (s + n // 2 - 1) // (n // 2)
    return 2 * s * (2 * up - 1) - up


def comm_kernel(cfg, basis_ref, data_hbm, z_ref, gram_ref,
                xb, bb, zs, zr, ga_all, gb_all, q_all, ypart_all, ysib_all, ypair_all, yr_all, yfull_all,
                zp_all, sax_all, rax_all, say_all, ray_all, sby_all,
                rby_all, sbx_all, rbx_all, fin_all, zx_s_all, zx_r_all, xt,
                g1, r1, s1, r2, s2, r3, s3, a2, gfull,
                xsem, bsem, zsem, gsem, y_sems, ssem, zx_sem,
                m1, m2, m3, m4, m5, far_sem):
    X, Y, Z, ZL, ZH, C = cfg.X, cfg.Y, cfg.Z, cfg.ZL, cfg.ZH, cfg.C
    FS = cfg.FS
    OWN, A, NC, CW = cfg.OWN, cfg.alpha, cfg.NC, cfg.CW
    dp = lax.axis_index("dp")
    feat = lax.axis_index("feat")
    my = dp % Y
    mx = (dp // Y) % X
    zl = dp // (X * Y)
    mc = feat % C
    mz = (feat // C) * ZL + zl
    me = {"x": mx, "y": my}

    def dev(ox=0, oy=0, oz=0, oc=0):
        x = (mx + ox + X) % X
        y = (my + oy + Y) % Y
        z = (mz + oz + Z) % Z
        c = (mc + oc) % C
        return {"dp": ((z % ZL) * X + x) * Y + y, "feat": (z // ZL) * C + c}

    partner = dev(oz=1 - 2 * zl)

    def rdma(src, dst, ssem, rsem, device):
        return pltpu.make_async_remote_copy(
            src_ref=src, dst_ref=dst, send_sem=ssem, recv_sem=rsem,
            device_id=device, device_id_type=MESH,
        )

    load = pltpu.make_async_copy(data_hbm, xb, xsem)
    load.start()

    fetch = pltpu.make_async_copy(basis_ref, bb, bsem)
    fetch.start()
    xc = [(ox, oc) for ox in range(X) for oc in range(C) if (ox, oc) != (0, 0)]
    peers = {(o % X, 0, 0, 0) for o in range(1, X)}
    peers |= {(0, o % Y, 0, 0) for o in (1, 2, -1, -2)}
    peers |= {(0, 0, o % Z, 0) for o in (ZL, -ZL) if o % Z}
    peers |= {(0, 0, 0, oc) for oc in range(1, C)}
    barrier = pltpu.get_barrier_semaphore()
    pl.semaphore_signal(barrier, inc=1, device_id=partner, device_id_type=MESH)
    for peer in sorted(peers):
        pl.semaphore_signal(barrier, inc=1, device_id=dev(*peer), device_id_type=MESH)
    fetch.wait()
    own = bb[0].astype(BF16).astype(F32)
    zs[...] = jnp.concatenate([own, jnp.zeros((64 - OWN, cfg.K), F32)], axis=0).astype(BF16)
    pl.semaphore_wait(barrier, len(peers) + 1)

    swap = rdma(zs, zr, zsem.at[0], zsem.at[1], partner)
    swap.start()
    if ZH > 1:
        pl.semaphore_signal(far_sem, inc=1, device_id=dev(oz=ZL), device_id_type=MESH)
    swap.wait_recv()
    other = zr[...].astype(F32)[:OWN]
    unit = jnp.concatenate(
        [jnp.where(zl == 0, own, other), jnp.where(zl == 0, other, own)], axis=0
    ).astype(BF16)
    pos = lambda h: position(h, Y)
    for c in range(NC):
        ga_all[c, mx, 0] = unit[:A, c * CW:(c + 1) * CW]
        gb_all[c, my, mx] = unit[A:, c * CW:(c + 1) * CW]
    pending = [swap]
    ring = lambda n: sorted(range(1, n), key=lambda o: -min(o, n - o))
    xo = ring(X)
    ta, tb = cfg.trees[:2]
    order = sorted(ta, key=pos)
    cuts = [(0, 0), (1, 1), (2, 2), (3, 3), (4, Y)]
    groups = [[h for h in [0] + order if lo <= abs(h) <= hi] for lo, hi in cuts]
    groups = [h for h in groups if h]
    first = [n for n in range(1, len(groups)) if abs(groups[n][0]) <= 2]
    later = [n for n in range(1, len(groups)) if abs(groups[n][0]) > 2]
    far = [h for n in later for h in groups[n]]

    def below(t, h):
        return sorted([k for k, v in t.items() if v == h], key=lambda k: -abs(k))

    def send(src, dst, sems, i, device):
        cp = rdma(src, dst, sems.at[0, i], sems.at[1, i], device)
        cp.start()
        pending.append(cp)

    def arrived(dst, sems, i):
        rdma(dst, dst, sems.at[0, i], sems.at[1, i], partner).wait_recv()

    def flush():
        while pending:
            pending.pop().wait_send()

    def span(group):
        return pl.ds(pos(group[0]), len(group))

    def gather(c):
        ga, gb = ga_all.at[c], gb_all.at[c]
        ax, ay, bx, by = [gsem.at[c, i] for i in range(4)]

        def along_y_a(h):
            for k in below(ta, h):
                send(ga.at[mx, pos(h)], ga.at[mx, pos(k)], ay, pos(k), dev(oy=k - h))

        def along_x_a(n):
            part = ga.at[mx, span(groups[n])]
            for i, o in enumerate(xo):
                if n in relayed and o == X // 2:
                    continue
                send(part, part, ax, n * X + i, dev(ox=o))

        relayed = [n for n in (0, 1) if X == 4 and n in [0] + first]
        went = set()

        def wait_x_a(n, o):
            if (n, o) not in went:
                arrived(ga.at[(mx - o + X) % X, span(groups[n])], ax, n * X + xo.index(o))
                went.add((n, o))

        def relay(n):
            o = 1 if n % 2 == 0 else X - 1
            wait_x_a(n, o)
            part = ga.at[(mx - o + X) % X, span(groups[n])]
            send(part, part, ax, n * X + xo.index(X // 2), dev(ox=o))

        def along_y_b(h):
            part = gb.at[(my - h + Y) % Y]
            for k in below(tb, h):
                send(part, part, by, pos(k), dev(oy=k - h))

        def wait_b(h):
            arrived(gb.at[(my - h + Y) % Y], by, pos(h))

        along_y_a(0)
        for i, o in enumerate(xo):
            send(gb.at[my, mx], gb.at[my, mx], bx, i, dev(ox=o))
        along_x_a(0)
        yield 3.5
        for i, o in enumerate(xo):
            arrived(gb.at[my, (mx - o + X) % X], bx, i)
        along_y_b(0)
        yield 4.5
        for n in first:
            for h in groups[n]:
                arrived(ga.at[mx, pos(h)], ay, pos(h))
                along_y_a(h)
            along_x_a(n)
        yield 8
        for n in first[::-1]:
            for h in groups[n]:
                wait_b(h)
                along_y_b(h)
        for n in relayed:
            relay(n)
        yield 8.5
        for n in later:
            for h in groups[n]:
                arrived(ga.at[mx, pos(h)], ay, pos(h))
            along_x_a(n)
        yield 12
        for h in far:
            wait_b(h)
        for n in range(len(groups)):
            for o in xo:
                wait_x_a(n, o)

    def arrange(c):
        ga, gb, q = ga_all.at[c], gb_all.at[c], q_all.at[c]

        def pair(i, carry):
            ux = i // (Y // 2)
            uy = (i % (Y // 2)) * 2
            a, b = [
                jnp.concatenate([ga[ux, pos(my - v + Y)].astype(F32), gb[v, ux].astype(F32)], axis=0)
                for v in (uy, uy + 1)
            ]
            for zz in range(ZL):
                rows = jnp.concatenate(
                    [a[zz * OWN:(zz + 1) * OWN], b[zz * OWN:(zz + 1) * OWN]], axis=0
                ).astype(BF16)
                at = pl.multiple_of(((zz * X + ux) * Y + uy) * OWN, 2 * OWN)
                q[pl.ds(at, 2 * OWN)] = rows
            return carry
        lax.fori_loop(0, X * Y // 2, pair, 0)

    TS = cfg.T // cfg.FE

    def sum_y(c):
        ypart, ysib, ypair = ypart_all.at[c], ysib_all.at[c], ypair_all.at[c]
        yr, yfull, q, y_sem = yr_all.at[c], yfull_all.at[c], q_all.at[c], y_sems.at[c]
        part = jnp.dot(xb[...], q[...], preferred_element_type=F32).astype(BF16)
        for h in range(C):
            for k in range(ZH):
                lo = (h * ZH + k) * TS
                ypart[h, k] = part[lo:lo + TS]
        mh = mz // ZL
        for h in range(1, C):
            cp = rdma(ypart.at[(mc + h) % C], ysib, y_sem.at[0, 0], y_sem.at[1, 0],
                      dev(oc=h))
            cp.start()
            pending.append(cp)
            yield 15
            cp.wait_recv()
        pair = ypart[mc].astype(F32) + ysib[...].astype(F32)
        ypair[...] = pair.astype(BF16)
        zoff = [ZL * o for o in ring(ZH)]
        if zoff:
            pl.semaphore_wait(far_sem, 1)
        for i, oz in enumerate(zoff):
            to = (mz + oz) % Z // ZL
            cp = rdma(ypair.at[to], yr.at[i], y_sem.at[0, 1 + i], y_sem.at[1, 1 + i],
                      dev(oz=oz))
            cp.start()
            pending.append(cp)
        flush()
        yield 20.5
        total = ypart[mc, mh].astype(F32) + ysib[mh].astype(F32)
        for i in range(len(zoff)):
            rdma(yr.at[i], yr.at[i], y_sem.at[0, 1 + i], y_sem.at[1, 1 + i],
                 partner).wait_recv()
            total = total + yr[i].astype(F32)
        yfull[mc, mh] = total.astype(BF16)
        slot = yfull.at[mc, mh]
        for i, oz in enumerate(zoff):
            cp = rdma(slot, slot, y_sem.at[2, 1 + i], y_sem.at[3, 1 + i], dev(oz=oz))
            cp.start()
            pending.append(cp)
        yield 26
        for i, oz in enumerate(zoff):
            slot = yfull.at[mc, (mz + Z - oz) % Z // ZL]
            rdma(slot, slot, y_sem.at[2, 1 + i], y_sem.at[3, 1 + i], partner).wait_recv()
        slot = yfull.at[mc]
        for h in range(1, C):
            cp = rdma(slot, slot, y_sem.at[2, 0], y_sem.at[3, 0], dev(oc=h))
            cp.start()
            pending.append(cp)
            yield 27.5
            slot = yfull.at[(mc + h) % C]
            rdma(slot, slot, y_sem.at[2, 0], y_sem.at[3, 0], dev(oc=h)).wait_recv()

    def product(c):
        y = yfull_all[c].reshape(cfg.T, CW)
        tile = 2 * OWN * (4 if FS % (8 * OWN) == 0 else 1)

        def one(i, carry):
            rows = pl.ds(pl.multiple_of(i * tile, tile), tile)
            zp_all[c, rows] = jnp.dot(xt[rows], y, preferred_element_type=F32)
            return carry
        lax.fori_loop(0, FS // tile, one, 0)

    def turn(n, of):
        def one(i, carry):
            rows = pl.ds(pl.multiple_of(i * 128, 128), 128)
            xt[rows] = xb[:, rows].T
            return carry
        tiles = FS // 128
        lax.fori_loop(n * tiles // of, (n + 1) * tiles // of, one, 0)

    def scatter(c):
        ta, tb = cfg.trees[2:]
        zp, fin, zx_s, zx_r = zp_all.at[c], fin_all.at[c], zx_s_all.at[c], zx_r_all.at[c]
        sax, rax, say, ray = sax_all.at[c], rax_all.at[c], say_all.at[c], ray_all.at[c]
        sby, rby, sbx, rbx = sby_all.at[c], rby_all.at[c], sbx_all.at[c], rbx_all.at[c]
        ax, ay, bx, by = [ssem.at[c, i] for i in range(4)]

        def rows_a(hx, hy):
            u = ((mx - hx + X) % X) * Y + (my - hy + Y) % Y
            at0 = pl.multiple_of(u * OWN, OWN)
            at1 = pl.multiple_of((X * Y + u) * OWN, OWN)
            return jnp.concatenate([zp[pl.ds(at0, OWN)], zp[pl.ds(at1, A - OWN)]], axis=0)

        def rows_b(hx, hy):
            u = ((mx - hx + X) % X) * Y + (my - hy + Y) % Y
            return zp[pl.ds(pl.multiple_of((X * Y + u) * OWN + (A - OWN), 8), cfg.beta)]

        def out_x_a(n):
            for i, o in enumerate(xo):
                for h in groups[n]:
                    sax[i, pos(h)] = rows_a(o, h).astype(BF16)
                part = span(groups[n])
                send(sax.at[i, part], rax.at[i, part], ax, n * X + i, dev(ox=-o))

        def out_y_b(h):
            for hx in range(X):
                v = rows_b(hx, h)
                for k in below(tb, h):
                    v = v + rby[pos(k), hx].astype(F32)
                sby[pos(h), hx] = v.astype(BF16)
            send(sby.at[pos(h)], rby.at[pos(h)], by, pos(h), dev(oy=tb[h] - h))

        def sum_a(h):
            v = rows_a(0, h)
            for i in range(len(xo)):
                v = v + rax[i, pos(h)].astype(F32)
            for k in below(ta, h):
                v = v + ray[pos(k)].astype(F32)
            return v

        def out_y_a(h):
            say[pos(h)] = sum_a(h).astype(BF16)
            send(say.at[pos(h)], ray.at[pos(h)], ay, pos(h), dev(oy=ta[h] - h))

        def wait_x_a(n):
            for i in range(len(xo)):
                arrived(rax.at[i, span(groups[n])], ax, n * X + i)

        def wait_y(buf, sems, t, h):
            for k in below(t, h):
                arrived(buf.at[pos(k)], sems, pos(k))

        for n in later:
            out_x_a(n)
        for h in far:
            out_y_b(h)
        for n in first[::-1]:
            out_x_a(n)
            for h in groups[n]:
                if not below(tb, h):
                    out_y_b(h)
        out_x_a(0)
        yield 34
        for n in first[::-1]:
            for h in groups[n]:
                if below(tb, h):
                    wait_y(rby, by, tb, h)
                    out_y_b(h)
        yield 35
        for n in later:
            wait_x_a(n)
        for h in far:
            out_y_a(h)
        yield 36
        for n in first[::-1]:
            wait_x_a(n)
            for h in groups[n]:
                if below(ta, h):
                    wait_y(ray, ay, ta, h)
                out_y_a(h)
        yield 38.5
        wait_y(rby, by, tb, 0)
        for i, o in enumerate([0] + xo):
            v = rows_b(o, 0)
            for k in below(tb, 0):
                v = v + rby[pos(k), o].astype(F32)
            if o == 0:
                last_b = v
            else:
                sbx[i - 1] = v.astype(BF16)
                send(sbx.at[i - 1], rbx.at[i - 1], bx, i - 1, dev(ox=-o))
        yield 41
        wait_x_a(0)
        wait_y(ray, ay, ta, 0)
        fin[pl.ds(0, A)] = sum_a(0)
        for i in range(len(xo)):
            arrived(rbx.at[i], bx, i)
            last_b = last_b + rbx[i].astype(F32)
        fin[pl.ds(A, cfg.beta)] = last_b
        lo = fin[pl.ds(0, OWN)]
        hi = fin[pl.ds(OWN, OWN)]
        zx_s[...] = jnp.concatenate(
            [jnp.where(zl == 0, hi, lo), jnp.zeros((64 - OWN, CW), F32)], axis=0
        ).astype(BF16)
        cp = rdma(zx_s, zx_r, zx_sem.at[c, 0], zx_sem.at[c, 1], partner)
        cp.start()
        pending.append(cp)
        flush()
        yield 45
        cp.wait_recv()
        z_ref[:, c * CW:(c + 1) * CW] = (
            (jnp.where(zl == 0, lo, hi) + zx_r[...].astype(F32)[:OWN]) / float(cfg.TOTAL_T)
        )

    def gram_sum(z):
        h, m, l = split3(jnp.concatenate([z, jnp.zeros((64 - OWN, cfg.K), F32)], axis=0))
        gl = lax.dot_general(
            jnp.concatenate([h, h, m, m, h, l], axis=0), jnp.concatenate([h, m, h, m, l, h], axis=0),
            (((0,), (0,)), ((), ())), preferred_element_type=F32,
        )
        g1[0] = gl[:, :128]
        g1[1] = gl[:, 128:]
        RX, RZ = cfg.RX, cfg.RZ
        m = mc * X + mx

        def exchange(offs, sems, src, dst, wait):
            copies = []
            for i, off in enumerate(offs):
                cp = rdma(src(off), dst(i), sems.at[0, i], sems.at[1, i], dev(*off))
                cp.start()
                copies.append(cp)
            flush()
            for i, off in reversed(list(enumerate(offs))):
                back = wait(i, off)
                rdma(back, back, sems.at[0, i], sems.at[1, i], dev(*off)).wait_recv()
            pending.extend(copies)

        xoff = [(ox, 0, 0, oc) for ox in xo + [0] for oc in range(C) if (ox, oc) != (0, 0)]
        zoff = [(0, 0, oz, 0) for oz in ring(Z)]
        yoff = [(0, oy, 0, 0) for oy in ring(Y)]

        def rows1(off):
            t = ((mc + off[3]) % C) * X + (mx + off[0] + X) % X
            return pl.ds(pl.multiple_of(t * RX, RX), RX)

        mine = pl.ds(pl.multiple_of(m * RX, RX), RX)
        exchange(xoff, m1, lambda off: g1.at[:, rows1(off)], lambda i: r1.at[i], lambda i, off: r1.at[i])
        total = g1[:, mine]
        for i in range(len(xoff)):
            total = total + r1[i]
        s1[...] = total

        def tile(z):
            return z % 2, pl.ds(pl.multiple_of((z // 2) * RZ, RZ), RZ)

        def tile_to(off):
            return tile((mz + off[2] + Z) % Z)

        exchange(zoff, m2, lambda off: s1.at[tile_to(off)], lambda i: r2.at[i], lambda i, off: r2.at[i])
        half, rows = tile(mz)
        total = s1[half, rows]
        for i in range(len(zoff)):
            total = total + r2[i]
        s2[...] = total
        exchange(yoff, m3, lambda off: s2, lambda i: r3.at[i], lambda i, off: r3.at[i])
        total = s2[...]
        for i in range(len(yoff)):
            total = total + r3[i]
        a2[half, rows] = total
        own_tile = a2.at[half, rows]
        exchange(zoff, m4, lambda off: own_tile, lambda i: own_tile,
                 lambda i, off: a2.at[tile((mz - off[2] + Z) % Z)])
        gfull[:, mine] = a2[...]
        near = [off for off in xoff if off[3] == 0]
        exchange(near, m5, lambda off: a2, lambda i: gfull.at[:, mine],
                 lambda i, off: gfull.at[:, rows1((-off[0], 0, 0, 0))])
        for h in range(1, C):
            def half(c):
                return gfull.at[:, pl.ds(pl.multiple_of(c % C * (X * RX), X * RX), X * RX)]
            cp = rdma(half(mc), half(mc), m5.at[0, len(near)], m5.at[1, len(near)], dev(oc=h))
            cp.start()
            pending.append(cp)
            rdma(half(mc + h), half(mc + h), m5.at[0, len(near)], m5.at[1, len(near)],
                 dev(oc=h)).wait_recv()
        gram_ref[...] = gfull[...]

    def chain(c):
        yield from gather(c)
        arrange(c)
        yield from sum_y(c)
        product(c)
        yield from scatter(c)

    def turns(of):
        load.wait()
        for n in range(of):
            yield TURN + 0.5 * n
            turn(n, of)

    running = [[0.0, c, chain(c)] for c in range(NC)] + [[TURN, NC, turns(4)]]
    while running:
        running.sort(key=lambda r: r[:2])
        step = running[0]
        try:
            step[0] = next(step[2]) + (LATER * step[1] if step[1] < NC else 0)
        except StopIteration:
            running.remove(step)
    gram_sum(z_ref[...])
    flush()


def communicate(cfg, basis, data, vmem=48 << 20):
    X, Y, Z, C, ZH = cfg.X, cfg.Y, cfg.Z, cfg.C, cfg.ZH
    K, OWN, T, FS, A, B = cfg.K, cfg.OWN, cfg.T, cfg.FS, cfg.alpha, cfg.beta
    TS, N, W = T // cfg.FE, cfg.NC, cfg.CW
    nx, nz, ny = cfg.MX - 1, Z - 1, Y - 1
    VM = pltpu.VMEM
    DMA = pltpu.SemaphoreType.DMA
    scratch = [
        VM((T, FS), BF16), VM((1, OWN, K), F32), VM((64, K), BF16), VM((64, K), BF16),
        VM((N, X, Y, A, W), BF16), VM((N, Y, X, B, W), BF16), VM((N, FS, W), BF16),
        VM((N, C, ZH, TS, W), BF16), VM((N, ZH, TS, W), BF16), VM((N, ZH, TS, W), BF16),
        VM((N, ZH, TS, W), BF16), VM((N, C, ZH, TS, W), BF16),
        VM((N, FS, W), F32), VM((N, X - 1, Y, A, W), BF16), VM((N, X - 1, Y, A, W), BF16),
        VM((N, Y, A, W), BF16), VM((N, Y, A, W), BF16),
        VM((N, Y, X, B, W), BF16), VM((N, Y, X, B, W), BF16),
        VM((N, X - 1, B, W), BF16), VM((N, X - 1, B, W), BF16),
        VM((N, 2 * OWN, W), F32), VM((N, 64, W), BF16), VM((N, 64, W), BF16), VM((FS, T), BF16),
        VM((2, K, 128), F32), VM((nx, 2, cfg.RX, 128), F32), VM((2, cfg.RX, 128), F32),
        VM((nz, cfg.RZ, 128), F32), VM((cfg.RZ, 128), F32), VM((ny, cfg.RZ, 128), F32),
        VM((cfg.RZ, 128), F32), VM((2, cfg.RX, 128), F32), VM((2, K, 128), F32),
        DMA, DMA, DMA((2,)), DMA((N, 4, 2, 5 * X)), DMA((N, 4, 1 + ZH)),
        DMA((N, 4, 2, 5 * X)), DMA((N, 2)),
        DMA((2, nx)), DMA((2, nz)), DMA((2, ny)), DMA((2, nz)), DMA((2, nx)),
        pltpu.SemaphoreType.REGULAR,
    ]

    def body(*refs):
        comm_kernel(cfg, *refs)

    return pl.pallas_call(
        body,
        out_shape=(
            jax.ShapeDtypeStruct((OWN, K), F32),
            jax.ShapeDtypeStruct((2, K, 128), F32),
        ),
        in_specs=[pl.BlockSpec(memory_space=pltpu.HBM)] * 2,
        out_specs=(pl.BlockSpec(memory_space=pltpu.VMEM), pl.BlockSpec(memory_space=pltpu.VMEM)),
        scratch_shapes=scratch,
        compiler_params=pltpu.CompilerParams(
            collective_id=0, has_side_effects=True, vmem_limit_bytes=vmem
        ),
        name="power_step",
    )(
        pltpu.with_memory_space_constraint(basis, pltpu.HBM),
        pltpu.with_memory_space_constraint(data, pltpu.HBM),
    )


def split3(v):
    h = v.astype(BF16)
    r = v - h.astype(F32)
    m = r.astype(BF16)
    return h, m, (r - m.astype(F32)).astype(BF16)


def factor_kernel(scale, B, z_ref, gram_ref, out_ref, w):
    own, K = z_ref.shape
    w[:, 0:128] = gram_ref[0] * scale
    w[:, 128:256] = gram_ref[1] * scale
    w[:, 256:384] = jnp.concatenate([z_ref[...], jnp.zeros((128 - own, K), F32)], axis=0).T
    sub = lax.broadcasted_iota(jnp.int32, (8, 128), 0)
    G = B // 8
    for blk in range(K // B):
        r0 = blk * B
        t0 = r0 // 128
        tiles = list(range(t0, 3))
        v = [[w[r0 + 8 * s:r0 + 8 * s + 8, t * 128:(t + 1) * 128] for t in tiles] for s in range(G)]
        scales = []
        for s0 in range(G):
            lane = (r0 + 8 * s0) % 128
            col = {
                s: [jnp.broadcast_to(v[s][0][:, lane + k:lane + k + 1], (8, 128)) for k in range(8)]
                for s in range(s0, G)
            }
            dvec = jnp.zeros((8, 128), F32)
            for j in range(8):
                prow = [jnp.broadcast_to(v[s0][t][j:j + 1], (8, 128)) for t in range(len(tiles))]
                pcol = [jnp.broadcast_to(col[s0][k][j:j + 1], (8, 128)) if k >= j else None
                        for k in range(8)]
                inv = 1.0 / pcol[j]
                dvec = jnp.where(sub == j, pcol[j], dvec)
                for s in range(s0, G):
                    mult = col[s][j] * inv
                    if s == s0:
                        mult = jnp.where(sub > j, mult, 0.0)
                    for k in range(j + 1, 8):
                        col[s][k] = col[s][k] - mult * pcol[k]
                    for t in range(len(tiles)):
                        v[s][t] = v[s][t] - mult * prow[t]
            scales.append(lax.rsqrt(dvec))
        for s in range(G):
            for t in range(len(tiles)):
                v[s][t] = v[s][t] * scales[s]
                if tiles[t] == 2:
                    w[r0 + 8 * s:r0 + 8 * s + 8, 256:384] = v[s][t]
        if blk + 1 < K // B:
            rows = jnp.concatenate([jnp.concatenate(v[s], axis=1) for s in range(G)], axis=0)
            h, m, l = split3(rows)
            n0 = ((r0 + B) // 128) * 128 - t0 * 128
            left = jnp.concatenate([h, h, m, m, h, l], axis=0)
            right = jnp.concatenate([h, m, h, m, l, h], axis=0)
            upd = lax.dot_general(left[:, n0:K - t0 * 128], right[:, n0:], (((0,), (0,)), ((), ())),
                                  preferred_element_type=F32)
            c0 = t0 * 128 + n0
            w[r0 + B:K, c0:384] = w[r0 + B:K, c0:384] - upd[r0 + B - c0:]
    out_ref[0] = w[:, 256:384].T[:own]


def factor(cfg, z, gram, block=32):
    def body(z_ref, gram_ref, out_ref, w):
        factor_kernel(1.0 / float(cfg.F), block, z_ref, gram_ref, out_ref, w)

    return pl.pallas_call(
        body,
        out_shape=jax.ShapeDtypeStruct((1, cfg.OWN, cfg.K), F32),
        in_specs=[pl.BlockSpec(memory_space=pltpu.VMEM)] * 2,
        out_specs=pl.BlockSpec(memory_space=pltpu.VMEM),
        scratch_shapes=[pltpu.VMEM((cfg.K, 384), F32)],
        compiler_params=pltpu.CompilerParams(vmem_limit_bytes=8 << 20),
        name="factor_rows",
    )(z, gram)


def solution(mesh):
    cfg = Cfg(zl=2, x=4, y=8, zh=4, core=2, tokens=512)

    def per_device(data, basis):
        z, gram = communicate(cfg, basis, data)
        return factor(cfg, z, gram)

    return jax.shard_map(
        per_device, mesh=mesh, in_specs=(P("dp", "feat"), P("feat", "dp", None)),
        out_specs=P("feat", "dp", None), check_vma=False,
    )
```
